32 devices in a mesh: leaf: 8 (over y, x, core), col: 4 (over z).
Axes of the slice: x: 2, y: 2, z: 4, core: 2. Of those that a mesh axis runs over, the one named last changes fastest.
Arguments:
- right_sides: float32 [256, 16384], P('col', 'leaf'), may hold values from -6 to 6
- inverse_first: float32 [32, 128, 128], P('leaf'), may hold values from -0.5 to 0.5
- coupling_first: float32 [32, 3, 128, 128], P('leaf'), may hold values from -0.3125 to 0.3125
- links_first: int32 [32, 3], P('leaf'), may hold values from 0 to 11, as said below
- order_first: int32 [8, 12], P('leaf'), may hold values from 0 to 11, as said below
- inverse_second: float32 [32, 128, 128], P('leaf'), may hold values from -0.5 to 0.5
- coupling_second: float32 [32, 3, 128, 128], P('leaf'), may hold values from -0.3125 to 0.3125
- links_second: int32 [32, 3], P('leaf'), may hold values from 0 to 7, as said below
- order_second: int32 [8, 8], P('leaf'), may hold values from 0 to 7, as said below
- inverse_third: float32 [32, 128, 128], P('leaf'), may hold values from -0.5 to 0.5
- coupling_third: float32 [32, 3, 128, 128], P('leaf'), may hold values from -0.3125 to 0.3125
- links_third: int32 [32, 3], P('leaf'), may hold values from 0 to 3, as said below
- order_third: int32 [8, 4], P('leaf'), may hold values from 0 to 3, as said below
- front_rows: int32 [3, 8], P(None, 'leaf'), may hold values from 128 to 512
- root_inverse: float32 [2, 2048, 2048], P(None, 'leaf', 'col'), may hold values from -0.125 to 0.125
- root_coupling: float32 [2048, 2048], P('leaf', 'col'), may hold values from -0.125 to 0.125
Outputs:
- solved_first: float32 [256, 4096], P('col', 'leaf')
- solved_second: float32 [256, 4096], P('col', 'leaf')
- solved_third: float32 [256, 4096], P('col', 'leaf')
- root_solution: float32 [256, 2, 2048], P('col', None, 'leaf')
The draws below stay inside these ranges and needn't reach their ends.
Inputs may be any that keep to these rules, and one draw needn't show every extreme that they name: `links_first`: each row names 3 different skeleton blocks of its front. `links_second`: each row names 3 different skeleton blocks of its front. `links_third`: each row names 3 different skeleton blocks of its front. `order_first`: each row is a permutation. `order_second`: each row is a permutation. `order_third`: each row is a permutation.
All inputs are finite; a program needn't handle non-finite values.
Results may differ from the reference program's by a relative error of at most 0.0003.
Values sent between devices are 32-bit elements; how exact they have to be, the bound alone decides.
No kernel may reach another device: no remote copies, remote signals or barrier semaphores. Data moves between devices by JAX's collectives and lax.ppermute only.
A program may use at most 64 MiB of HBM per device.

```python
import jax
import jax.numpy as jnp
from jax import lax

BLK = 128
RED = 4
NSK = 3
SKEL2 = 4
LEVELS = 3
NPAN = 2
NRHS = 256
SKEL1 = 8
SKEL0 = 12
SECTION0 = 16
FRONTS = 8
PANEL_ROWS = 256
PANEL = 2048


def pick_links(key, row_total, choice_total):
    scores = jax.random.randint(key, (row_total, choice_total), 0, 65536) * choice_total + jnp.arange(choice_total, dtype=jnp.int32)[None, :]
    ranking = jnp.argsort(scores, axis=1)
    return ranking[:, :NSK].astype(jnp.int32)


def pick_orders(key, choice_total):
    scores = jax.random.randint(key, (FRONTS, choice_total), 0, 65536) * choice_total + jnp.arange(choice_total, dtype=jnp.int32)[None, :]
    return jnp.argsort(scores, axis=1).astype(jnp.int32)


def draw_links_first(key, part):
    return pick_links(jax.random.fold_in(key, 11), FRONTS * RED, SKEL0)


def draw_links_second(key, part):
    return pick_links(jax.random.fold_in(key, 12), FRONTS * RED, SKEL1)


def draw_links_third(key, part):
    return pick_links(jax.random.fold_in(key, 13), FRONTS * RED, SKEL2)


def draw_order_first(key, part):
    return pick_orders(jax.random.fold_in(key, 21), SKEL0)


def draw_order_second(key, part):
    return pick_orders(jax.random.fold_in(key, 22), SKEL1)


def draw_order_third(key, part):
    return pick_orders(jax.random.fold_in(key, 23), SKEL2)


def draw_front_rows(key, part):
    largest_rows = RED * BLK
    fewest_rows = largest_rows // 4
    values = jax.random.randint(jax.random.fold_in(key, 31), (LEVELS, FRONTS), fewest_rows, largest_rows + 1)
    chosen_fronts = jax.random.randint(jax.random.fold_in(key, 32), (LEVELS,), 0, FRONTS)
    front_slots = jnp.arange(FRONTS, dtype=jnp.int32)[None, :]
    values = jnp.where(front_slots == chosen_fronts[:, None], largest_rows, values)
    values = jnp.where(front_slots == (chosen_fronts[:, None] + 1) % FRONTS, fewest_rows, values)
    return values.astype(jnp.int32)


def steps_of(stream_key, shape, cuts, low, top_value):
    factor_of, own = 1.0, jax.random.fold_in(stream_key, 6)
    for axis_at, blocks in cuts:
        heights = jnp.exp(jax.random.uniform(jax.random.fold_in(own, axis_at), (blocks,), jnp.float32, low / len(cuts), top_value / len(cuts)))
        factor_of = factor_of * jnp.repeat(heights, shape[axis_at] // blocks).reshape([-1 if axis == axis_at else 1 for axis in range(len(shape))])
    return factor_of


def centred(own_key, dims, width, bound, cuts=(), kind=jnp.bfloat16):
    result = width * jax.random.normal(own_key, dims, jnp.float32)
    if cuts:
        result = result * steps_of(own_key, dims, cuts, -0.22, 0.18)
    return jnp.clip(result, -bound, bound).astype(kind)


def setup_inputs(seed: int = 0) -> dict:
    arg_keys = jax.random.split(jax.random.key(seed), 17)
    return {
        "right_sides": centred(arg_keys[0], (NRHS, FRONTS * SECTION0 * BLK), 1.0, 6.0, ((0, 4), (1, 8)), jnp.float32),
        "inverse_first": centred(arg_keys[1], (FRONTS * RED, BLK, BLK), BLK ** -0.5, 0.5, ((0, 8),), jnp.float32),
        "coupling_first": centred(arg_keys[2], (FRONTS * RED, NSK, BLK, BLK), (NSK * BLK) ** -0.5, 0.3125, ((0, 8),), jnp.float32),
        "links_first": draw_links_first(jax.random.fold_in(arg_keys[16], 71), 0),
        "order_first": draw_order_first(jax.random.fold_in(arg_keys[16], 71), 0),
        "inverse_second": centred(arg_keys[5], (FRONTS * RED, BLK, BLK), BLK ** -0.5, 0.5, ((0, 8),), jnp.float32),
        "coupling_second": centred(arg_keys[6], (FRONTS * RED, NSK, BLK, BLK), (NSK * BLK) ** -0.5, 0.3125, ((0, 8),), jnp.float32),
        "links_second": draw_links_second(jax.random.fold_in(arg_keys[16], 71), 0),
        "order_second": draw_order_second(jax.random.fold_in(arg_keys[16], 71), 0),
        "inverse_third": centred(arg_keys[9], (FRONTS * RED, BLK, BLK), BLK ** -0.5, 0.5, ((0, 8),), jnp.float32),
        "coupling_third": centred(arg_keys[10], (FRONTS * RED, NSK, BLK, BLK), (NSK * BLK) ** -0.5, 0.3125, ((0, 8),), jnp.float32),
        "links_third": draw_links_third(jax.random.fold_in(arg_keys[16], 71), 0),
        "order_third": draw_order_third(jax.random.fold_in(arg_keys[16], 71), 0),
        "front_rows": draw_front_rows(jax.random.fold_in(arg_keys[16], 71), 0),
        "root_inverse": centred(arg_keys[14], (NPAN, PANEL, PANEL), PANEL ** -0.5, 0.125, ((1, 8), (2, 4)), jnp.float32),
        "root_coupling": centred(arg_keys[15], (PANEL, PANEL), PANEL ** -0.5, 0.125, ((0, 8), (1, 4)), jnp.float32),
    }


def product(left_side, right_side):
    return jnp.dot(left_side, right_side, precision=lax.Precision.HIGHEST, preferred_element_type=jnp.float32)


def eliminate(section, inverse, coupling, link_ids, live_count):
    skeleton_count = section.shape[2] - RED
    positions = jnp.arange(RED, dtype=jnp.int32)[:, None] * BLK + jnp.arange(BLK, dtype=jnp.int32)[None, :]
    live_rows = (positions[None, :, :] < live_count[:, None, None]).astype(jnp.float32)
    redundant = section[:, :, :RED] * live_rows[None]
    solved = jnp.einsum("rfib,fiba->rfia", redundant, inverse, precision=lax.Precision.HIGHEST) * live_rows[None]
    pushed = jnp.einsum("rfia,fikab->rfikb", solved, coupling, precision=lax.Precision.HIGHEST)
    targets = (link_ids[:, :, :, None] == jnp.arange(skeleton_count, dtype=jnp.int32)).astype(jnp.float32)
    update = jnp.einsum("rfikb,fiks->rfsb", pushed, targets, precision=lax.Precision.HIGHEST)
    return solved, section[:, :, RED:] - update


def join_halves(skeleton, level_index):
    half_blocks = skeleton.shape[2] // 2
    fronts_all = jnp.arange(FRONTS, dtype=jnp.int32)
    upper_half = (fronts_all >> level_index) & 1
    lower_front = fronts_all - upper_half * (2 ** level_index)
    upper_front = lower_front + 2 ** level_index
    split = skeleton.reshape(skeleton.shape[0], FRONTS, 2, half_blocks, BLK)
    first_part = split[:, lower_front, upper_half]
    second_part = split[:, upper_front, upper_half]
    return jnp.concatenate([first_part, second_part], 2)


def reference(right_sides, inverse_first, coupling_first, links_first, order_first, inverse_second, coupling_second, links_second, order_second, inverse_third, coupling_third, links_third, order_third, front_rows, root_inverse, root_coupling):
    section = right_sides.reshape(NRHS, FRONTS, SECTION0, BLK)
    level_data = ((inverse_first, coupling_first, links_first, order_first), (inverse_second, coupling_second, links_second, order_second), (inverse_third, coupling_third, links_third, order_third))
    outputs = []
    for level_index in range(3):
        inverse, coupling, link_ids, order_map = level_data[level_index]
        solved, skeleton = eliminate(section, inverse.reshape(FRONTS, RED, BLK, BLK), coupling.reshape(FRONTS, RED, NSK, BLK, BLK), link_ids.reshape(FRONTS, RED, NSK), front_rows[level_index])
        outputs.append(solved.reshape(NRHS, FRONTS * RED * BLK))
        if level_index < 2:
            skeleton = join_halves(skeleton, level_index)
        section = jnp.take_along_axis(skeleton, order_map[None, :, :, None], axis=2)
    root_rhs = section.reshape(NRHS, FRONTS, NPAN, PANEL_ROWS).transpose(0, 2, 1, 3).reshape(NRHS, NPAN, PANEL)
    first_solve = product(root_rhs[:, 0], root_inverse[0])
    coupled = product(first_solve, root_coupling)
    second_solve = product(root_rhs[:, 1] - coupled, root_inverse[1])
    last_panel = product(second_solve, root_inverse[1].T)
    back_coupled = product(last_panel, root_coupling.T)
    first_panel = product(first_solve - back_coupled, root_inverse[0].T)
    root_solution = jnp.stack([first_panel, last_panel], 1)
    return (outputs[0], outputs[1], outputs[2], root_solution)
```

```python
import functools

import jax
import jax.numpy as jnp
from jax import lax
from jax.experimental import pallas as pl
from jax.experimental.pallas import tpu as pltpu
from jax.sharding import PartitionSpec as P


def partner(block, axis, stride):
    count = lax.axis_size(axis)
    route = []
    for low in range(count):
        high = low | 1 << stride
        if high != low and high < count:
            route += [(low, high), (high, low)]
    return lax.ppermute(block, axis, route)


def eliminate(section, inverse, coupling, link_ids, live_count):
    block_rows = inverse.shape[-1]
    red_blocks = inverse.shape[0]
    link_total = coupling.shape[1]
    rhs_rows = section.shape[0]
    skeleton_count = section.shape[1] // block_rows - red_blocks
    redundant = section[:, : red_blocks * block_rows].reshape(rhs_rows, red_blocks, block_rows)
    positions = lax.broadcasted_iota(
        jnp.int32, (red_blocks, block_rows), 0
    ) * block_rows + lax.broadcasted_iota(jnp.int32, (red_blocks, block_rows), 1)
    live_rows = (positions < live_count).astype(jnp.float32)
    solved = (
        jnp.einsum("rib,iba->ria", redundant * live_rows, inverse, precision=lax.Precision.HIGHEST)
        * live_rows
    )
    pushed = jnp.einsum("ria,ikab->rikb", solved, coupling, precision=lax.Precision.HIGHEST)
    targets = (
        link_ids[:, :, None]
        == lax.broadcasted_iota(jnp.int32, (red_blocks, link_total, skeleton_count), 2)
    ).astype(jnp.float32)
    update = jnp.einsum("rikb,iks->rsb", pushed, targets, precision=lax.Precision.HIGHEST)
    skeleton = (
        section[:, red_blocks * block_rows :].reshape(rhs_rows, skeleton_count, block_rows) - update
    )
    return (solved.reshape(rhs_rows, red_blocks * block_rows), skeleton)


def join_halves(skeleton, level_index):
    half_blocks = skeleton.shape[1] // 2
    upper_half = lax.axis_index("leaf") >> level_index & 1
    kept_half = lax.dynamic_slice_in_dim(skeleton, upper_half * half_blocks, half_blocks, 1)
    sent_half = lax.dynamic_slice_in_dim(skeleton, (1 - upper_half) * half_blocks, half_blocks, 1)
    received = partner(sent_half, "leaf", level_index)
    return jnp.where(
        upper_half == 0,
        jnp.concatenate([kept_half, received], 1),
        jnp.concatenate([received, kept_half], 1),
    )


def spread_columns(values):
    return lax.all_gather(values, "col", axis=0, tiled=True)


def spread_leaf(values):
    return lax.all_gather(values, "leaf", axis=0, tiled=True)


def to_leaf_rows(values):
    full_rows = lax.all_gather(values, "col", axis=1, tiled=True)
    return lax.all_to_all(full_rows, "leaf", split_axis=1, concat_axis=0, tiled=True)


def to_column_rows(values):
    full_rows = lax.all_gather(values, "leaf", axis=1, tiled=True)
    return lax.all_to_all(full_rows, "col", split_axis=1, concat_axis=0, tiled=True)


def forward_product(values, matrix):
    return lax.psum_scatter(
        jnp.dot(
            values, matrix, precision=lax.Precision.HIGHEST, preferred_element_type=jnp.float32
        ),
        "leaf",
        scatter_dimension=0,
        tiled=True,
    )


def backward_product(values, matrix):
    return lax.psum_scatter(
        lax.dot_general(
            values,
            matrix,
            (((1,), (1,)), ((), ())),
            precision=lax.Precision.HIGHEST,
            preferred_element_type=jnp.float32,
        ),
        "col",
        scatter_dimension=0,
        tiled=True,
    )


def root_wide(section, root_inverse, root_coupling):
    rhs_rows = section.shape[0]
    panel_count = root_inverse.shape[0]
    panel_rows = root_inverse.shape[1]
    root_rhs = section.reshape(rhs_rows, panel_count, panel_rows)
    full_rhs = spread_columns(root_rhs)
    first_solve = forward_product(full_rhs[:, 0], root_inverse[0])
    coupled = forward_product(to_leaf_rows(first_solve), root_coupling)
    second_solve = forward_product(full_rhs[:, 1] - to_leaf_rows(coupled), root_inverse[1])
    forward_both = spread_leaf(jnp.stack([first_solve, second_solve], 1))
    last_panel = backward_product(forward_both[:, 1], root_inverse[1])
    back_coupled = backward_product(to_column_rows(last_panel), root_coupling)
    first_panel = backward_product(
        forward_both[:, 0] - to_column_rows(back_coupled), root_inverse[0]
    )
    root_solution = jnp.stack([first_panel, last_panel], 1)
    return root_solution


def flip(block, axis, distance):
    count = lax.axis_size(axis)
    return lax.ppermute(block, axis, [(i, i ^ distance) for i in range(count)])


def swap_columns(parts):
    return [parts[0]] + [flip(parts[e], "col", e) for e in range(1, len(parts))]


def kernel_call(body, out_shapes, *operands):
    spec = pl.BlockSpec(memory_space=pltpu.VMEM)
    smem = pl.BlockSpec(memory_space=pltpu.SMEM)
    return pl.pallas_call(
        body,
        out_shape=[jax.ShapeDtypeStruct(s, d) for s, d in out_shapes],
        in_specs=[smem] + [spec] * (len(operands) - 1),
        out_specs=[spec] * len(out_shapes),
        compiler_params=pltpu.CompilerParams(vmem_limit_bytes=40 * 1024 * 1024),
    )(*operands)


def halves(values):
    high = values.astype(jnp.bfloat16)
    return high, (values - high.astype(jnp.float32)).astype(jnp.bfloat16)


def product(values, high, low, contract):
    rows = values.shape[0]
    own_high, own_low = halves(values)
    dims = (((1,), (contract,)), ((), ()))
    both = lax.dot_general(
        jnp.concatenate([own_high, own_low], 0), high, dims, preferred_element_type=jnp.float32
    )
    cross = lax.dot_general(own_high, low, dims, preferred_element_type=jnp.float32)
    return both[:rows] + both[rows:] + cross


def regroup(values, distance, parts):
    if distance == 0:
        return values
    size = values.shape[0] // parts
    return jnp.concatenate(
        [values[(d ^ distance) * size : (d ^ distance) * size + size] for d in range(parts)], 0
    )


def span(index, size):
    return pl.ds(pl.multiple_of(index * size, size), size)


def assemble_kernel(place, *refs):
    pieces, (high, low) = refs[:-2], refs[-2:]
    leaf = place[0]
    offset = 0
    for (distance, start), piece in zip(PIECES, pieces, strict=True):
        rows = piece.shape[0]
        block_rows = pieces[0].shape[0]
        first = (leaf ^ distance) * block_rows + start * rows
        where = pl.ds(pl.multiple_of(first, rows), rows)
        part_high, part_low = halves(piece[...])
        high[where, :] = part_high
        low[where, :] = part_low


PIECES = tuple(
    (plane | core, start) for core in (0, 1) for plane, start in ((0, 0), (2, 0), (4, 0), (6, 0), (6, 1))
)


def spread_matrix(place, block):
    half = block.shape[0] // 2
    near = flip(block, "leaf", 2)
    far = flip(block, "leaf", 4)
    pieces = [block, near, far, flip(near[:half], "leaf", 4), flip(far[half:], "leaf", 2)]
    pieces += [flip(piece, "leaf", 1) for piece in pieces]
    shape = (block.shape[0] * lax.axis_size("leaf"), block.shape[1])
    return kernel_call(assemble_kernel, [(shape, jnp.bfloat16)] * 2, place, *pieces)


def arrange_kernel(place, values, *parts):
    leaf_count, _, rows, width = values.shape
    total = leaf_count * width
    own_width = parts[0].shape[1] - total
    fronts = own_width // width
    for e, part in enumerate(parts):
        for leaf in range(leaf_count):
            part[:, leaf * width : (leaf + 1) * width] = values[leaf, 0]
        for j in range(fronts):
            part[:, total + j * width : total + (j + 1) * width] = values[
                (place[1] ^ e) * fronts + j, 1
            ]


def first_kernel(place, *refs):
    parts, (high, low, first, rest) = refs[:-4], refs[-4:]
    total = high.shape[0]
    values = jnp.concatenate([part[:, :total] for part in parts], 0)
    rest[...] = jnp.concatenate([part[:, total:] for part in parts], 0)
    first[...] = product(values, high[...], low[...], 0)


def gathered_product(place, parts, high, low):
    count = len(parts)
    width = parts[0].shape[1]
    total = None
    for e, part in enumerate(parts):
        rows = span(place[1] ^ e, width)
        term = product(regroup(part[...], e, count), high[rows, :], low[rows, :], 0)
        total = term if total is None else total + term
    return total


def coupled_kernel(place, *refs):
    parts, (high, low, rest, result) = refs[:-4], refs[-4:]
    result[...] = rest[...] - gathered_product(place, parts, high, low)


def scatter_product(place, values, high, low, sent):
    count = len(sent)
    width = sent[0].shape[1]
    for e, part in enumerate(sent):
        rows = span(place[1] ^ e, width)
        part[...] = regroup(product(values, high[rows, :], low[rows, :], 1), e, count)


def turn_kernel(place, *refs):
    count = (len(refs) - 2) // 2
    parts, (high, low), sent = refs[:count], refs[count : count + 2], refs[count + 2 :]
    second = gathered_product(place, parts, high, low)
    scatter_product(place, second, high, low, sent)


def back_kernel(place, *refs):
    count = (len(refs) - 3) // 2
    parts, (high, low), last, sent = (
        refs[:count],
        refs[count : count + 2],
        refs[count + 2],
        refs[count + 3 :],
    )
    total = sum(part[...] for part in parts[1:]) + parts[0][...]
    last[...] = total
    scatter_product(place, total, high, low, sent)


def final_kernel(place, *refs):
    count = (len(refs) - 4) // 2
    parts = refs[:count]
    high, low, first, last = refs[count : count + 4]
    sent = refs[count + 4 :]
    total = first[...] - (sum(part[...] for part in parts[1:]) + parts[0][...])
    solved = product(total, high[...], low[...], 1)
    size = total.shape[0] // count
    for e, part in enumerate(sent):
        part[...] = jnp.concatenate(
            [solved[e * size : (e + 1) * size], last[e * size : (e + 1) * size, :]], 1
        )


def collect_kernel(place, *refs):
    parts, result = refs[:-1], refs[-1]
    leaf_count, _, rows, width = result.shape
    total = leaf_count * width
    fronts = (parts[0].shape[1] - total) // width
    for leaf in range(leaf_count):
        where = slice(leaf * width, (leaf + 1) * width)
        result[leaf, 0] = sum(part[:, where] for part in parts[1:]) + parts[0][:, where]
    for e, part in enumerate(parts):
        for j in range(fronts):
            start = total + j * width
            result[(place[1] ^ e) * fronts + j, 1] = part[:, start : start + width]


def root_replicated(section, root_inverse, root_coupling):
    leaf_count, col_count = lax.axis_size("leaf"), lax.axis_size("col")
    place = jnp.stack([lax.axis_index("leaf"), lax.axis_index("col")]).astype(jnp.int32)
    first_high, first_low = spread_matrix(place, root_inverse[0])
    between_high, between_low = spread_matrix(place, root_coupling)
    second_high, second_low = spread_matrix(place, root_inverse[1])
    rhs_rows = section.shape[0]
    panel_count, panel_rows, own_columns = root_inverse.shape
    rows = rhs_rows // leaf_count
    group = rows * col_count
    total = panel_rows * leaf_count
    split = section.reshape(leaf_count, rows, panel_count, panel_rows).transpose(0, 2, 1, 3)
    whole = lax.all_to_all(split, "leaf", 0, 0, tiled=True)
    wide = [((rows, total + own_columns), jnp.float32)] * col_count
    one = ((group, own_columns), jnp.float32)
    parts = swap_columns(kernel_call(arrange_kernel, wide, place, whole))
    first, rest = kernel_call(first_kernel, [one, one], place, *parts, first_high, first_low)
    parts = swap_columns([first] * col_count)
    (left,) = kernel_call(coupled_kernel, [one], place, *parts, between_high, between_low, rest)
    parts = swap_columns([left] * col_count)
    parts = kernel_call(turn_kernel, [one] * col_count, place, *parts, second_high, second_low)
    parts = swap_columns(parts)
    last, *parts = kernel_call(
        back_kernel, [one] * (col_count + 1), place, *parts, between_high, between_low
    )
    parts = swap_columns(parts)
    parts = kernel_call(
        final_kernel, wide, place, *parts, first_high, first_low, first, last
    )
    parts = swap_columns(parts)
    (split,) = kernel_call(
        collect_kernel, [((leaf_count, panel_count, rows, panel_rows), jnp.float32)], place, *parts
    )
    whole = lax.all_to_all(split, "leaf", 0, 0, tiled=True)
    return whole.transpose(0, 2, 1, 3).reshape(rhs_rows, panel_count, panel_rows)


def replicates(rhs_rows, root_inverse):
    leaf_count, col_count = lax.axis_size("leaf"), lax.axis_size("col")
    panel_rows, own_columns = root_inverse.shape[1:]
    return (
        leaf_count == 8
        and col_count & (col_count - 1) == 0
        and rhs_rows % (8 * leaf_count) == 0
        and own_columns % panel_rows == 0
    )


def local(
    right_sides,
    inverse_first,
    coupling_first,
    links_first,
    order_first,
    inverse_second,
    coupling_second,
    links_second,
    order_second,
    inverse_third,
    coupling_third,
    links_third,
    order_third,
    front_rows,
    root_inverse,
    root_coupling,
):
    level_data = (
        (inverse_first, coupling_first, links_first, order_first),
        (inverse_second, coupling_second, links_second, order_second),
        (inverse_third, coupling_third, links_third, order_third),
    )
    section = right_sides
    outputs = []
    for level_index in range(3):
        inverse, coupling, link_ids, order_map = level_data[level_index]
        solved, skeleton = eliminate(
            section, inverse, coupling, link_ids, front_rows[level_index, 0]
        )
        outputs.append(solved)
        if level_index < 2:
            skeleton = join_halves(skeleton, level_index)
        skeleton = jnp.take(skeleton, order_map[0], axis=1)
        section = skeleton.reshape(skeleton.shape[0], -1)
    solve = root_replicated if replicates(right_sides.shape[0], root_inverse) else root_wide
    return (*outputs, solve(section, root_inverse, root_coupling))


def solution(mesh):
    in_specs = (
        P("col", "leaf"),
        P("leaf", None, None),
        P("leaf", None, None, None),
        P("leaf", None),
        P("leaf", None),
        P("leaf", None, None),
        P("leaf", None, None, None),
        P("leaf", None),
        P("leaf", None),
        P("leaf", None, None),
        P("leaf", None, None, None),
        P("leaf", None),
        P("leaf", None),
        P(None, "leaf"),
        P(None, "leaf", "col"),
        P("leaf", "col"),
    )
    out_specs = (P("col", "leaf"), P("col", "leaf"), P("col", "leaf"), P("col", None, "leaf"))
    return jax.shard_map(local, mesh=mesh, in_specs=in_specs, out_specs=out_specs, check_vma=False)
```

```python
import functools

import jax
import jax.numpy as jnp
from jax import lax
from jax.experimental import pallas as pl
from jax.experimental.pallas import tpu as pltpu
from jax.sharding import PartitionSpec as P


def partner(block, axis, stride):
    count = lax.axis_size(axis)
    route = []
    for low in range(count):
        high = low | 1 << stride
        if high != low and high < count:
            route += [(low, high), (high, low)]
    return lax.ppermute(block, axis, route)


def eliminate(section, inverse, coupling, link_ids, live_count):
    block_rows = inverse.shape[-1]
    red_blocks = inverse.shape[0]
    link_total = coupling.shape[1]
    rhs_rows = section.shape[0]
    skeleton_count = section.shape[1] // block_rows - red_blocks
    redundant = section[:, : red_blocks * block_rows].reshape(rhs_rows, red_blocks, block_rows)
    positions = lax.broadcasted_iota(
        jnp.int32, (red_blocks, block_rows), 0
    ) * block_rows + lax.broadcasted_iota(jnp.int32, (red_blocks, block_rows), 1)
    live_rows = (positions < live_count).astype(jnp.float32)
    solved = (
        jnp.einsum("rib,iba->ria", redundant * live_rows, inverse, precision=lax.Precision.HIGHEST)
        * live_rows
    )
    pushed = jnp.einsum("ria,ikab->rikb", solved, coupling, precision=lax.Precision.HIGHEST)
    targets = (
        link_ids[:, :, None]
        == lax.broadcasted_iota(jnp.int32, (red_blocks, link_total, skeleton_count), 2)
    ).astype(jnp.float32)
    update = jnp.einsum("rikb,iks->rsb", pushed, targets, precision=lax.Precision.HIGHEST)
    skeleton = (
        section[:, red_blocks * block_rows :].reshape(rhs_rows, skeleton_count, block_rows) - update
    )
    return (solved.reshape(rhs_rows, red_blocks * block_rows), skeleton)


def join_halves(skeleton, level_index):
    half_blocks = skeleton.shape[1] // 2
    upper_half = lax.axis_index("leaf") >> level_index & 1
    kept_half = lax.dynamic_slice_in_dim(skeleton, upper_half * half_blocks, half_blocks, 1)
    sent_half = lax.dynamic_slice_in_dim(skeleton, (1 - upper_half) * half_blocks, half_blocks, 1)
    received = partner(sent_half, "leaf", level_index)
    return jnp.where(
        upper_half == 0,
        jnp.concatenate([kept_half, received], 1),
        jnp.concatenate([received, kept_half], 1),
    )


def spread_columns(values):
    return lax.all_gather(values, "col", axis=0, tiled=True)


def spread_leaf(values):
    return lax.all_gather(values, "leaf", axis=0, tiled=True)


def to_leaf_rows(values):
    full_rows = lax.all_gather(values, "col", axis=1, tiled=True)
    return lax.all_to_all(full_rows, "leaf", split_axis=1, concat_axis=0, tiled=True)


def to_column_rows(values):
    full_rows = lax.all_gather(values, "leaf", axis=1, tiled=True)
    return lax.all_to_all(full_rows, "col", split_axis=1, concat_axis=0, tiled=True)


def forward_product(values, matrix):
    return lax.psum_scatter(
        jnp.dot(
            values, matrix, precision=lax.Precision.HIGHEST, preferred_element_type=jnp.float32
        ),
        "leaf",
        scatter_dimension=0,
        tiled=True,
    )


def backward_product(values, matrix):
    return lax.psum_scatter(
        lax.dot_general(
            values,
            matrix,
            (((1,), (1,)), ((), ())),
            precision=lax.Precision.HIGHEST,
            preferred_element_type=jnp.float32,
        ),
        "col",
        scatter_dimension=0,
        tiled=True,
    )


def root_wide(section, root_inverse, root_coupling):
    rhs_rows = section.shape[0]
    panel_count = root_inverse.shape[0]
    panel_rows = root_inverse.shape[1]
    root_rhs = section.reshape(rhs_rows, panel_count, panel_rows)
    full_rhs = spread_columns(root_rhs)
    first_solve = forward_product(full_rhs[:, 0], root_inverse[0])
    coupled = forward_product(to_leaf_rows(first_solve), root_coupling)
    second_solve = forward_product(full_rhs[:, 1] - to_leaf_rows(coupled), root_inverse[1])
    forward_both = spread_leaf(jnp.stack([first_solve, second_solve], 1))
    last_panel = backward_product(forward_both[:, 1], root_inverse[1])
    back_coupled = backward_product(to_column_rows(last_panel), root_coupling)
    first_panel = backward_product(
        forward_both[:, 0] - to_column_rows(back_coupled), root_inverse[0]
    )
    root_solution = jnp.stack([first_panel, last_panel], 1)
    return root_solution


def flip(block, axis, distance):
    count = lax.axis_size(axis)
    return lax.ppermute(block, axis, [(i, i ^ distance) for i in range(count)])


def swap_columns(parts):
    return [parts[0]] + [flip(parts[e], "col", e) for e in range(1, len(parts))]


def kernel_call(body, out_shapes, scalars, operands, held=(), scratch=()):
    spec = pl.BlockSpec(memory_space=pltpu.VMEM)
    smem = pl.BlockSpec(memory_space=pltpu.SMEM)
    used = len(scalars) + len(operands)

    def run(*refs):
        body(*refs[:used], *refs[used + len(held) :])

    return pl.pallas_call(
        run,
        out_shape=[jax.ShapeDtypeStruct(shape, kind) for shape, kind in out_shapes],
        in_specs=[smem] * len(scalars)
        + [spec] * len(operands)
        + [pl.BlockSpec(memory_space=pl.ANY)] * len(held),
        out_specs=[spec] * len(out_shapes),
        scratch_shapes=list(scratch),
        compiler_params=pltpu.CompilerParams(vmem_limit_bytes=40 * 1024 * 1024),
    )(*scalars, *operands, *held)


def halves(values):
    high = values.astype(jnp.bfloat16)
    return high, (values - high.astype(jnp.float32)).astype(jnp.bfloat16)


def product(values, high, low, contract):
    rows = values.shape[0]
    own_high, own_low = halves(values)
    dims = (((1,), (contract,)), ((), ()))
    both = lax.dot_general(
        jnp.concatenate([own_high, own_low], 0), high, dims, preferred_element_type=jnp.float32
    )
    cross = lax.dot_general(own_high, low, dims, preferred_element_type=jnp.float32)
    return both[:rows] + both[rows:] + cross


def regroup(values, distance, parts):
    if distance == 0:
        return values
    size = values.shape[0] // parts
    return jnp.concatenate(
        [values[(d ^ distance) * size : (d ^ distance) * size + size] for d in range(parts)], 0
    )


def span(index, size):
    return pl.ds(pl.multiple_of(index * size, size), size)


def assemble_kernel(place, *refs):
    pieces, (high, low) = refs[:-2], refs[-2:]
    leaf = place[0]
    offset = 0
    for (distance, start), piece in zip(PIECES, pieces, strict=True):
        rows = piece.shape[0]
        block_rows = pieces[0].shape[0]
        first = (leaf ^ distance) * block_rows + start * rows
        where = pl.ds(pl.multiple_of(first, rows), rows)
        part_high, part_low = halves(piece[...])
        high[where, :] = part_high
        low[where, :] = part_low


PIECES = tuple(
    (plane | core, start) for core in (0, 1) for plane, start in ((0, 0), (2, 0), (4, 0), (6, 0), (6, 1))
)


def spread_matrix(place, block):
    half = block.shape[0] // 2
    near = flip(block, "leaf", 2)
    far = flip(block, "leaf", 4)
    pieces = [block, near, far, flip(near[:half], "leaf", 4), flip(far[half:], "leaf", 2)]
    pieces += [flip(piece, "leaf", 1) for piece in pieces]
    shape = (block.shape[0] * lax.axis_size("leaf"), block.shape[1])
    return kernel_call(assemble_kernel, [(shape, jnp.bfloat16)] * 2, [place], pieces)


def arrange_kernel(place, values, *parts):
    leaf_count, _, rows, width = values.shape
    total = leaf_count * width
    own_width = parts[0].shape[1] - total
    fronts = own_width // width
    for e, part in enumerate(parts):
        for leaf in range(leaf_count):
            part[:, leaf * width : (leaf + 1) * width] = values[leaf, 0]
        for j in range(fronts):
            part[:, total + j * width : total + (j + 1) * width] = values[
                (place[1] ^ e) * fronts + j, 1
            ]


def first_kernel(place, *refs):
    parts, (high, low, first, rest) = refs[:-4], refs[-4:]
    total = high.shape[0]
    values = jnp.concatenate([part[:, :total] for part in parts], 0)
    rest[...] = jnp.concatenate([part[:, total:] for part in parts], 0)
    first[...] = product(values, high[...], low[...], 0)


def gathered_product(place, parts, high, low):
    count = len(parts)
    width = parts[0].shape[1]
    total = None
    for e, part in enumerate(parts):
        rows = span(place[1] ^ e, width)
        term = product(regroup(part[...], e, count), high[rows, :], low[rows, :], 0)
        total = term if total is None else total + term
    return total


def coupled_kernel(place, *refs):
    parts, (high, low, rest, result) = refs[:-4], refs[-4:]
    result[...] = rest[...] - gathered_product(place, parts, high, low)


def scatter_product(place, values, high, low, sent):
    count = len(sent)
    width = sent[0].shape[1]
    for e, part in enumerate(sent):
        rows = span(place[1] ^ e, width)
        part[...] = regroup(product(values, high[rows, :], low[rows, :], 1), e, count)


def turn_kernel(place, *refs):
    count = (len(refs) - 2) // 2
    parts, (high, low), sent = refs[:count], refs[count : count + 2], refs[count + 2 :]
    second = gathered_product(place, parts, high, low)
    scatter_product(place, second, high, low, sent)


def back_kernel(place, *refs):
    count = (len(refs) - 3) // 2
    parts, (high, low), last, sent = (
        refs[:count],
        refs[count : count + 2],
        refs[count + 2],
        refs[count + 3 :],
    )
    total = sum(part[...] for part in parts[1:]) + parts[0][...]
    last[...] = total
    scatter_product(place, total, high, low, sent)


def final_kernel(place, *refs):
    count = (len(refs) - 4) // 2
    parts = refs[:count]
    high, low, first, last = refs[count : count + 4]
    sent = refs[count + 4 :]
    total = first[...] - (sum(part[...] for part in parts[1:]) + parts[0][...])
    solved = product(total, high[...], low[...], 1)
    size = total.shape[0] // count
    for e, part in enumerate(sent):
        part[...] = jnp.concatenate(
            [solved[e * size : (e + 1) * size], last[e * size : (e + 1) * size, :]], 1
        )


def collect_kernel(place, *refs):
    parts, result = refs[:-1], refs[-1]
    leaf_count, _, rows, width = result.shape
    total = leaf_count * width
    fronts = (parts[0].shape[1] - total) // width
    for leaf in range(leaf_count):
        where = slice(leaf * width, (leaf + 1) * width)
        result[leaf, 0] = sum(part[:, where] for part in parts[1:]) + parts[0][:, where]
    for e, part in enumerate(parts):
        for j in range(fronts):
            start = total + j * width
            result[(place[1] ^ e) * fronts + j, 1] = part[:, start : start + width]


def reduce_blocks(level, live, links, blocks, inverse, coupling, solved):
    red_blocks, link_total, size = inverse.shape[0], coupling.shape[1], inverse.shape[1]
    lanes = lax.broadcasted_iota(jnp.int32, (1, size), 1)
    for i in range(red_blocks):
        mask = (lanes + i * size < live[level, 0]).astype(jnp.float32)
        high, low = halves(inverse[i])
        value = product(blocks[i] * mask, high, low, 0) * mask
        solved[:, i * size : (i + 1) * size] = value
        pairs = [halves(coupling[i, k]) for k in range(link_total)]
        high, low = (jnp.concatenate(part, 1) for part in zip(*pairs, strict=True))
        pushed = product(value, high, low, 0)
        for k in range(link_total):
            target = red_blocks + links[i, k]
            blocks[target] = blocks[target] - pushed[:, k * size : (k + 1) * size]


def send_halves(place, level, blocks, red_blocks, kept, sent):
    half = kept.shape[0]
    upper = (place[0] >> level) & 1
    kept[...] = blocks[pl.ds(red_blocks + upper * half, half)]
    sent[...] = blocks[pl.ds(red_blocks + (1 - upper) * half, half)]


def load_halves(place, level, order, kept, received, joined, blocks):
    half = kept.shape[0]
    upper = (place[0] >> level) & 1
    joined[pl.ds(upper * half, half)] = kept[...]
    joined[pl.ds((1 - upper) * half, half)] = received[...]
    for n in range(2 * half):
        blocks[n] = joined[order[0, n]]


def lowest_kernel(place, live, links, section, inverse, coupling, solved, kept, sent, blocks):
    size = inverse.shape[1]
    for n in range(blocks.shape[0]):
        blocks[n] = section[:, n * size : (n + 1) * size]
    reduce_blocks(0, live, links, blocks, inverse, coupling, solved)
    send_halves(place, 0, blocks, inverse.shape[0], kept, sent)


def middle_kernel(
    place, live, links, order, old, received, inverse, coupling, solved, kept, sent, joined, blocks
):
    load_halves(place, 0, order, old, received, joined, blocks)
    reduce_blocks(1, live, links, blocks, inverse, coupling, solved)
    send_halves(place, 1, blocks, inverse.shape[0], kept, sent)


def highest_kernel(
    place, live, links, order, last_order, old, received, inverse, coupling, solved, split, joined, blocks
):
    load_halves(place, 1, order, old, received, joined, blocks)
    reduce_blocks(2, live, links, blocks, inverse, coupling, solved)
    red_blocks, size = inverse.shape[0], inverse.shape[1]
    leaf_count, panel_count, rows, width = split.shape
    per_panel = width // size
    for panel in range(panel_count):
        for j in range(per_panel):
            block = blocks[red_blocks + last_order[0, panel * per_panel + j]]
            split[:, panel, :, j * size : (j + 1) * size] = block.reshape(leaf_count, rows, size)


def eliminate_all(place, right_sides, level_data, front_rows, panel_count, panel_rows):
    rhs_rows = right_sides.shape[0]
    red_blocks, size = level_data[0][0].shape[:2]
    leaf_count = lax.axis_size("leaf")
    one = ((rhs_rows, red_blocks * size), jnp.float32)

    def many(count):
        return (count, rhs_rows, size)

    inverse, coupling, links, order = level_data[0]
    count = right_sides.shape[1] // size
    half = ((count - red_blocks) // 2, rhs_rows, size)
    solved_first, kept, sent = kernel_call(
        lowest_kernel,
        [one, (half, jnp.float32), (half, jnp.float32)],
        [place, front_rows, links],
        [right_sides, inverse, coupling],
        scratch=[pltpu.VMEM(many(count), jnp.float32)],
    )
    received = flip(sent, "leaf", 1)
    inverse, coupling, links, next_order = level_data[1]
    count -= red_blocks
    half = ((count - red_blocks) // 2, rhs_rows, size)
    solved_second, kept, sent = kernel_call(
        middle_kernel,
        [one, (half, jnp.float32), (half, jnp.float32)],
        [place, front_rows, links, order],
        [kept, received, inverse, coupling],
        scratch=[pltpu.VMEM(many(count), jnp.float32)] * 2,
    )
    received = flip(sent, "leaf", 2)
    inverse, coupling, links, last_order = level_data[2]
    count -= red_blocks
    rows = rhs_rows // leaf_count
    solved_third, split = kernel_call(
        highest_kernel,
        [one, ((leaf_count, panel_count, rows, panel_rows), jnp.float32)],
        [place, front_rows, links, next_order, last_order],
        [kept, received, inverse, coupling],
        scratch=[pltpu.VMEM(many(count), jnp.float32)] * 2,
    )
    return (solved_first, solved_second, solved_third), split


def root_replicated(place, split, root_inverse, root_coupling):
    leaf_count, col_count = lax.axis_size("leaf"), lax.axis_size("col")
    first_high, first_low = spread_matrix(place, root_inverse[0])
    between_high, between_low = spread_matrix(place, root_coupling)
    second_high, second_low = spread_matrix(place, root_inverse[1])
    panel_count, panel_rows, own_columns = root_inverse.shape
    rows = split.shape[2]
    rhs_rows = rows * leaf_count
    group = rows * col_count
    total = panel_rows * leaf_count
    whole = lax.all_to_all(split, "leaf", 0, 0, tiled=True)
    wide = [((rows, total + own_columns), jnp.float32)] * col_count
    one = ((group, own_columns), jnp.float32)
    parts = swap_columns(kernel_call(arrange_kernel, wide, [place], [whole]))
    first, rest = kernel_call(
        first_kernel, [one, one], [place], [*parts, first_high, first_low]
    )
    parts = swap_columns([first] * col_count)
    (left,) = kernel_call(
        coupled_kernel, [one], [place], [*parts, between_high, between_low, rest]
    )
    parts = swap_columns([left] * col_count)
    parts = kernel_call(
        turn_kernel, [one] * col_count, [place], [*parts, second_high, second_low]
    )
    parts = swap_columns(parts)
    last, *parts = kernel_call(
        back_kernel, [one] * (col_count + 1), [place], [*parts, between_high, between_low]
    )
    parts = swap_columns(parts)
    parts = kernel_call(
        final_kernel, wide, [place], [*parts, first_high, first_low, first, last]
    )
    parts = swap_columns(parts)
    (split,) = kernel_call(
        collect_kernel,
        [((leaf_count, panel_count, rows, panel_rows), jnp.float32)],
        [place],
        parts,
    )
    whole = lax.all_to_all(split, "leaf", 0, 0, tiled=True)
    return whole.transpose(0, 2, 1, 3).reshape(rhs_rows, panel_count, panel_rows)


def replicates(rhs_rows, root_inverse):
    leaf_count, col_count = lax.axis_size("leaf"), lax.axis_size("col")
    panel_rows, own_columns = root_inverse.shape[1:]
    return (
        leaf_count == 8
        and col_count & (col_count - 1) == 0
        and rhs_rows % (8 * leaf_count) == 0
        and own_columns % panel_rows == 0
    )


def local(
    right_sides,
    inverse_first,
    coupling_first,
    links_first,
    order_first,
    inverse_second,
    coupling_second,
    links_second,
    order_second,
    inverse_third,
    coupling_third,
    links_third,
    order_third,
    front_rows,
    root_inverse,
    root_coupling,
):
    level_data = (
        (inverse_first, coupling_first, links_first, order_first),
        (inverse_second, coupling_second, links_second, order_second),
        (inverse_third, coupling_third, links_third, order_third),
    )
    if replicates(right_sides.shape[0], root_inverse):
        place = jnp.stack([lax.axis_index("leaf"), lax.axis_index("col")]).astype(jnp.int32)
        solved, split = eliminate_all(
            place, right_sides, level_data, front_rows, *root_inverse.shape[:2]
        )
        return (*solved, root_replicated(place, split, root_inverse, root_coupling))
    section = right_sides
    outputs = []
    for level_index in range(3):
        inverse, coupling, link_ids, order_map = level_data[level_index]
        solved, skeleton = eliminate(
            section, inverse, coupling, link_ids, front_rows[level_index, 0]
        )
        outputs.append(solved)
        if level_index < 2:
            skeleton = join_halves(skeleton, level_index)
        skeleton = jnp.take(skeleton, order_map[0], axis=1)
        section = skeleton.reshape(skeleton.shape[0], -1)
    return (*outputs, root_wide(section, root_inverse, root_coupling))


def solution(mesh):
    in_specs = (
        P("col", "leaf"),
        P("leaf", None, None),
        P("leaf", None, None, None),
        P("leaf", None),
        P("leaf", None),
        P("leaf", None, None),
        P("leaf", None, None, None),
        P("leaf", None),
        P("leaf", None),
        P("leaf", None, None),
        P("leaf", None, None, None),
        P("leaf", None),
        P("leaf", None),
        P(None, "leaf"),
        P(None, "leaf", "col"),
        P("leaf", "col"),
    )
    out_specs = (P("col", "leaf"), P("col", "leaf"), P("col", "leaf"), P("col", None, "leaf"))
    return jax.shard_map(local, mesh=mesh, in_specs=in_specs, out_specs=out_specs, check_vma=False)
```

```python
import functools

import jax
import jax.numpy as jnp
from jax import lax
from jax.experimental import pallas as pl
from jax.experimental.pallas import tpu as pltpu
from jax.sharding import PartitionSpec as P


def partner(block, axis, stride):
    count = lax.axis_size(axis)
    route = []
    for low in range(count):
        high = low | 1 << stride
        if high != low and high < count:
            route += [(low, high), (high, low)]
    return lax.ppermute(block, axis, route)


def eliminate(section, inverse, coupling, link_ids, live_count):
    block_rows = inverse.shape[-1]
    red_blocks = inverse.shape[0]
    link_total = coupling.shape[1]
    rhs_rows = section.shape[0]
    skeleton_count = section.shape[1] // block_rows - red_blocks
    redundant = section[:, : red_blocks * block_rows].reshape(rhs_rows, red_blocks, block_rows)
    positions = lax.broadcasted_iota(
        jnp.int32, (red_blocks, block_rows), 0
    ) * block_rows + lax.broadcasted_iota(jnp.int32, (red_blocks, block_rows), 1)
    live_rows = (positions < live_count).astype(jnp.float32)
    solved = (
        jnp.einsum("rib,iba->ria", redundant * live_rows, inverse, precision=lax.Precision.HIGHEST)
        * live_rows
    )
    pushed = jnp.einsum("ria,ikab->rikb", solved, coupling, precision=lax.Precision.HIGHEST)
    targets = (
        link_ids[:, :, None]
        == lax.broadcasted_iota(jnp.int32, (red_blocks, link_total, skeleton_count), 2)
    ).astype(jnp.float32)
    update = jnp.einsum("rikb,iks->rsb", pushed, targets, precision=lax.Precision.HIGHEST)
    skeleton = (
        section[:, red_blocks * block_rows :].reshape(rhs_rows, skeleton_count, block_rows) - update
    )
    return (solved.reshape(rhs_rows, red_blocks * block_rows), skeleton)


def join_halves(skeleton, level_index):
    half_blocks = skeleton.shape[1] // 2
    upper_half = lax.axis_index("leaf") >> level_index & 1
    kept_half = lax.dynamic_slice_in_dim(skeleton, upper_half * half_blocks, half_blocks, 1)
    sent_half = lax.dynamic_slice_in_dim(skeleton, (1 - upper_half) * half_blocks, half_blocks, 1)
    received = partner(sent_half, "leaf", level_index)
    return jnp.where(
        upper_half == 0,
        jnp.concatenate([kept_half, received], 1),
        jnp.concatenate([received, kept_half], 1),
    )


def spread_columns(values):
    return lax.all_gather(values, "col", axis=0, tiled=True)


def spread_leaf(values):
    return lax.all_gather(values, "leaf", axis=0, tiled=True)


def to_leaf_rows(values):
    full_rows = lax.all_gather(values, "col", axis=1, tiled=True)
    return lax.all_to_all(full_rows, "leaf", split_axis=1, concat_axis=0, tiled=True)


def to_column_rows(values):
    full_rows = lax.all_gather(values, "leaf", axis=1, tiled=True)
    return lax.all_to_all(full_rows, "col", split_axis=1, concat_axis=0, tiled=True)


def forward_product(values, matrix):
    return lax.psum_scatter(
        jnp.dot(
            values, matrix, precision=lax.Precision.HIGHEST, preferred_element_type=jnp.float32
        ),
        "leaf",
        scatter_dimension=0,
        tiled=True,
    )


def backward_product(values, matrix):
    return lax.psum_scatter(
        lax.dot_general(
            values,
            matrix,
            (((1,), (1,)), ((), ())),
            precision=lax.Precision.HIGHEST,
            preferred_element_type=jnp.float32,
        ),
        "col",
        scatter_dimension=0,
        tiled=True,
    )


def root_wide(section, root_inverse, root_coupling):
    rhs_rows = section.shape[0]
    panel_count = root_inverse.shape[0]
    panel_rows = root_inverse.shape[1]
    root_rhs = section.reshape(rhs_rows, panel_count, panel_rows)
    full_rhs = spread_columns(root_rhs)
    first_solve = forward_product(full_rhs[:, 0], root_inverse[0])
    coupled = forward_product(to_leaf_rows(first_solve), root_coupling)
    second_solve = forward_product(full_rhs[:, 1] - to_leaf_rows(coupled), root_inverse[1])
    forward_both = spread_leaf(jnp.stack([first_solve, second_solve], 1))
    last_panel = backward_product(forward_both[:, 1], root_inverse[1])
    back_coupled = backward_product(to_column_rows(last_panel), root_coupling)
    first_panel = backward_product(
        forward_both[:, 0] - to_column_rows(back_coupled), root_inverse[0]
    )
    root_solution = jnp.stack([first_panel, last_panel], 1)
    return root_solution


GROUP = 8


def flip(block, axis, distance):
    count = lax.axis_size(axis)
    return lax.ppermute(block, axis, [(i, i ^ distance) for i in range(count)])


def swap_columns(parts):
    return [parts[0]] + [flip(parts[e], "col", e) for e in range(1, len(parts))]


def kernel_call(body, out_shapes, scalars, operands, held=(), scratch=()):
    spec = pl.BlockSpec(memory_space=pltpu.VMEM)
    smem = pl.BlockSpec(memory_space=pltpu.SMEM)
    used = len(scalars) + len(operands)

    def run(*refs):
        body(*refs[:used], *refs[used + len(held) :])

    return pl.pallas_call(
        run,
        out_shape=[jax.ShapeDtypeStruct(shape, kind) for shape, kind in out_shapes],
        in_specs=[smem] * len(scalars)
        + [spec] * len(operands)
        + [pl.BlockSpec(memory_space=pl.ANY)] * len(held),
        out_specs=[spec] * len(out_shapes),
        scratch_shapes=list(scratch),
        compiler_params=pltpu.CompilerParams(vmem_limit_bytes=40 * 1024 * 1024),
    )(*scalars, *operands, *held)


def halves(values):
    high = values.astype(jnp.bfloat16)
    return high, (values - high.astype(jnp.float32)).astype(jnp.bfloat16)


def product(values, high, low, contract):
    rows = values.shape[0]
    own_high, own_low = halves(values)
    dims = (((1,), (contract,)), ((), ()))
    both = lax.dot_general(
        jnp.concatenate([own_high, own_low], 0), high, dims, preferred_element_type=jnp.float32
    )
    cross = lax.dot_general(own_high, low, dims, preferred_element_type=jnp.float32)
    return both[:rows] + both[rows:] + cross


def regroup(values, distance, parts):
    if distance == 0:
        return values
    size = values.shape[0] // parts
    return jnp.concatenate(
        [values[(d ^ distance) * size : (d ^ distance) * size + size] for d in range(parts)], 0
    )


def span(index, size):
    return pl.ds(pl.multiple_of(index * size, size), size)


def assemble_kernel(place, *refs):
    pieces, (high, low) = refs[:-2], refs[-2:]
    leaf = place[0]
    offset = 0
    for (distance, start), piece in zip(PIECES, pieces, strict=True):
        rows = piece.shape[0]
        block_rows = pieces[0].shape[0]
        first = (leaf ^ distance) * block_rows + start * rows
        where = pl.ds(pl.multiple_of(first, rows), rows)
        part_high, part_low = halves(piece[...])
        high[where, :] = part_high
        low[where, :] = part_low


PIECES = tuple(
    (plane | core, start) for core in (0, 1) for plane, start in ((0, 0), (2, 0), (4, 0), (6, 0), (6, 1))
)


def spread_matrix(place, block):
    half = block.shape[0] // 2
    near = flip(block, "leaf", 2)
    far = flip(block, "leaf", 4)
    pieces = [block, near, far, flip(near[:half], "leaf", 4), flip(far[half:], "leaf", 2)]
    pieces += [flip(piece, "leaf", 1) for piece in pieces]
    shape = (block.shape[0] * lax.axis_size("leaf"), block.shape[1])
    return kernel_call(assemble_kernel, [(shape, jnp.bfloat16)] * 2, [place], pieces)


def split_kernel(whole, high, low):
    high[...], low[...] = halves(whole[...])


def pair_kernel(own, other, high, low):
    rows = own.shape[0]
    high[:rows, :], low[:rows, :] = halves(own[...])
    high[rows:, :], low[rows:, :] = halves(other[...])


def first_kernel(place, *refs):
    count = (len(refs) - 5) // 2
    parts, (high, low, kept, received) = refs[:count], refs[count : count + 4]
    sent, pushed = refs[count + 4 : -1], refs[-1]
    rows, width = parts[0].shape
    values = product(jnp.concatenate([part[...] for part in parts], 0), high[...], low[...], 0)
    for e in range(count):
        pushed[e] = values[e * rows : (e + 1) * rows]
    chip, lower = place[0] >> 1, (place[0] & 1) == 0
    half = width // 2
    for f, part in enumerate(sent):
        where = span(chip ^ f, GROUP)
        for e in range(count):
            part[e * GROUP : (e + 1) * GROUP, :] = pushed[e, where, :]
        own, other = kept[where, half:], received[where, half:]
        part[rows:, :half] = jnp.where(lower, own, other)
        part[rows:, half:] = jnp.where(lower, other, own)


def share_kernel(place, *refs):
    count = (len(refs) - 1) // 2
    parts, sent, rest = refs[:count], refs[count:-1], refs[-1]
    rows = parts[0].shape[0] - GROUP
    total = sum(part[:rows, :] for part in parts[1:]) + parts[0][:rows, :]
    for f, part in enumerate(parts):
        rest[f] = part[rows:, :]
    for e, part in enumerate(sent):
        part[:rows, :] = total
        part[rows:, :] = rest[(place[0] >> 1) ^ place[1] ^ e]


def gathered_product(place, parts, high, low):
    count = len(parts)
    width = parts[0].shape[1]
    total = None
    for e, part in enumerate(parts):
        rows = span(place[1] ^ e, width)
        values = part[: count * GROUP, :]
        term = product(regroup(values, e, count), high[rows, :], low[rows, :], 0)
        total = term if total is None else total + term
    return total


def coupled_kernel(place, *refs):
    parts, (high, low, result) = refs[:-3], refs[-3:]
    rest = jnp.concatenate([part[len(parts) * GROUP :, :] for part in parts], 0)
    result[...] = rest - gathered_product(place, parts, high, low)


def scatter_product(place, values, high, low, sent):
    count = len(sent)
    width = sent[0].shape[1]
    for e, part in enumerate(sent):
        rows = span(place[1] ^ e, width)
        part[...] = regroup(product(values, high[rows, :], low[rows, :], 1), e, count)


def turn_kernel(place, *refs):
    count = (len(refs) - 2) // 2
    parts, (high, low), sent = refs[:count], refs[count : count + 2], refs[count + 2 :]
    second = gathered_product(place, parts, high, low)
    scatter_product(place, second, high, low, sent)


def back_kernel(place, *refs):
    count = (len(refs) - 3) // 2
    parts, (high, low), last, sent = (
        refs[:count],
        refs[count : count + 2],
        refs[count + 2],
        refs[count + 3 :],
    )
    total = sum(part[...] for part in parts[1:]) + parts[0][...]
    last[...] = total
    scatter_product(place, total, high, low, sent)


def final_kernel(place, *refs):
    count = (len(refs) - 4) // 2
    parts = refs[:count]
    high, low, first, last = refs[count : count + 4]
    sent = refs[count + 4 :]
    total = first[: last.shape[0], :] - (sum(part[...] for part in parts[1:]) + parts[0][...])
    solved = product(total, high[...], low[...], 1)
    size = total.shape[0] // count
    for e, part in enumerate(sent):
        part[...] = jnp.concatenate(
            [solved[e * size : (e + 1) * size], last[e * size : (e + 1) * size, :]], 1
        )


def collect_kernel(place, *refs):
    parts, result = refs[:-1], refs[-1]
    leaf_count, _, rows, width = result.shape
    total = leaf_count * width
    fronts = (parts[0].shape[1] - total) // width
    for leaf in range(leaf_count):
        where = slice(leaf * width, (leaf + 1) * width)
        result[leaf, 0] = sum(part[:, where] for part in parts[1:]) + parts[0][:, where]
    for e, part in enumerate(parts):
        for j in range(fronts):
            start = total + j * width
            result[(place[1] ^ e) * fronts + j, 1] = part[:, start : start + width]


def reduce_blocks(level, live, links, blocks, inverse, coupling, solved):
    red_blocks, link_total, size = inverse.shape[0], coupling.shape[1], inverse.shape[1]
    lanes = lax.broadcasted_iota(jnp.int32, (1, size), 1)
    for i in range(red_blocks):
        mask = (lanes + i * size < live[level, 0]).astype(jnp.float32)
        high, low = halves(inverse[i])
        value = product(blocks[i] * mask, high, low, 0) * mask
        solved[:, i * size : (i + 1) * size] = value
        pairs = [halves(coupling[i, k]) for k in range(link_total)]
        high, low = (jnp.concatenate(part, 1) for part in zip(*pairs, strict=True))
        pushed = product(value, high, low, 0)
        for k in range(link_total):
            target = red_blocks + links[i, k]
            blocks[target] = blocks[target] - pushed[:, k * size : (k + 1) * size]


def send_halves(place, level, blocks, red_blocks, kept, sent):
    half = kept.shape[0]
    upper = (place[0] >> level) & 1
    kept[...] = blocks[pl.ds(red_blocks + upper * half, half)]
    sent[...] = blocks[pl.ds(red_blocks + (1 - upper) * half, half)]


def load_halves(place, level, order, kept, received, joined, blocks):
    half = kept.shape[0]
    upper = (place[0] >> level) & 1
    joined[pl.ds(upper * half, half)] = kept[...]
    joined[pl.ds((1 - upper) * half, half)] = received[...]
    for n in range(2 * half):
        blocks[n] = joined[order[0, n]]


def lowest_kernel(place, live, links, section, inverse, coupling, solved, kept, sent, blocks):
    size = inverse.shape[1]
    for n in range(blocks.shape[0]):
        blocks[n] = section[:, n * size : (n + 1) * size]
    reduce_blocks(0, live, links, blocks, inverse, coupling, solved)
    send_halves(place, 0, blocks, inverse.shape[0], kept, sent)


def middle_kernel(
    place, live, links, order, old, received, inverse, coupling, solved, kept, sent, joined, blocks
):
    load_halves(place, 0, order, old, received, joined, blocks)
    reduce_blocks(1, live, links, blocks, inverse, coupling, solved)
    send_halves(place, 1, blocks, inverse.shape[0], kept, sent)


def highest_kernel(
    place, live, links, order, last_order, old, received, inverse, coupling, solved, kept, sent, joined, blocks
):
    load_halves(place, 1, order, old, received, joined, blocks)
    reduce_blocks(2, live, links, blocks, inverse, coupling, solved)
    red_blocks, size = inverse.shape[0], inverse.shape[1]
    core = place[0] & 1
    for n in range(blocks.shape[0] - red_blocks):
        block = red_blocks + last_order[0, n]
        columns = slice(n * size, (n + 1) * size)
        for chip in range(kept.shape[0] // GROUP):
            rows = slice(chip * GROUP, (chip + 1) * GROUP)
            kept[rows, columns] = blocks[block, span(2 * chip + core, GROUP), :]
            sent[rows, columns] = blocks[block, span(2 * chip + 1 - core, GROUP), :]


def eliminate_all(place, right_sides, level_data, front_rows):
    rhs_rows = right_sides.shape[0]
    red_blocks, size = level_data[0][0].shape[:2]
    one = ((rhs_rows, red_blocks * size), jnp.float32)

    def many(count):
        return (count, rhs_rows, size)

    inverse, coupling, links, order = level_data[0]
    count = right_sides.shape[1] // size
    half = ((count - red_blocks) // 2, rhs_rows, size)
    solved_first, kept, sent = kernel_call(
        lowest_kernel,
        [one, (half, jnp.float32), (half, jnp.float32)],
        [place, front_rows, links],
        [right_sides, inverse, coupling],
        scratch=[pltpu.VMEM(many(count), jnp.float32)],
    )
    received = flip(sent, "leaf", 1)
    inverse, coupling, links, next_order = level_data[1]
    count -= red_blocks
    half = ((count - red_blocks) // 2, rhs_rows, size)
    solved_second, kept, sent = kernel_call(
        middle_kernel,
        [one, (half, jnp.float32), (half, jnp.float32)],
        [place, front_rows, links, order],
        [kept, received, inverse, coupling],
        scratch=[pltpu.VMEM(many(count), jnp.float32)] * 2,
    )
    received = flip(sent, "leaf", 2)
    inverse, coupling, links, last_order = level_data[2]
    count -= red_blocks
    half = (rhs_rows // 2, (count - red_blocks) * size)
    solved_third, kept, sent = kernel_call(
        highest_kernel,
        [one, (half, jnp.float32), (half, jnp.float32)],
        [place, front_rows, links, next_order, last_order],
        [kept, received, inverse, coupling],
        scratch=[pltpu.VMEM(many(count), jnp.float32)] * 2,
    )
    return (solved_first, solved_second, solved_third), kept, flip(sent, "leaf", 1)


def root_replicated(place, kept, received, root_inverse, root_coupling):
    leaf_count, col_count = lax.axis_size("leaf"), lax.axis_size("col")
    panel_count, panel_rows, own_columns = root_inverse.shape
    group = GROUP * col_count
    total = panel_rows * leaf_count
    rhs_rows = GROUP * leaf_count
    pair = [((2 * panel_rows, own_columns), jnp.bfloat16)] * 2
    panel = [((total, own_columns), jnp.bfloat16)] * 2
    one = ((group, own_columns), jnp.float32)
    more = ((group + GROUP, own_columns), jnp.float32)
    wide = [((GROUP, total + own_columns), jnp.float32)] * col_count
    near_high, near_low = kernel_call(
        pair_kernel, pair, [], [root_inverse[0], flip(root_inverse[0], "leaf", 1)]
    )
    between = lax.all_gather(root_coupling, "leaf", axis=0, tiled=True)
    between_high, between_low = kernel_call(split_kernel, panel, [], [between])
    second_high, second_low = spread_matrix(place, root_inverse[1])
    first = lax.all_gather(root_inverse[0], "leaf", axis=0, tiled=True)
    first_high, first_low = kernel_call(split_kernel, panel, [], [first])
    joined = jnp.concatenate([kept[:, :panel_rows], received[:, :panel_rows]], 1)
    parts = swap_columns([joined] * col_count)
    parts = kernel_call(
        first_kernel,
        [more] * (leaf_count // 2),
        [place],
        [*parts, near_high, near_low, kept, received],
        scratch=[pltpu.VMEM((col_count, group, own_columns), jnp.float32)],
    )
    parts = [parts[0]] + [flip(parts[f], "leaf", 2 * f) for f in range(1, leaf_count // 2)]
    parts = kernel_call(
        share_kernel,
        [more] * col_count,
        [place],
        parts,
        scratch=[pltpu.VMEM((leaf_count // 2, GROUP, own_columns), jnp.float32)],
    )
    first_sum = parts[0]
    parts = swap_columns(parts)
    (left,) = kernel_call(coupled_kernel, [one], [place], [*parts, between_high, between_low])
    parts = swap_columns([left] * col_count)
    parts = kernel_call(
        turn_kernel, [one] * col_count, [place], [*parts, second_high, second_low]
    )
    parts = swap_columns(parts)
    last, *parts = kernel_call(
        back_kernel, [one] * (col_count + 1), [place], [*parts, between_high, between_low]
    )
    parts = swap_columns(parts)
    parts = kernel_call(
        final_kernel, wide, [place], [*parts, first_high, first_low, first_sum, last]
    )
    parts = swap_columns(parts)
    (split,) = kernel_call(
        collect_kernel,
        [((leaf_count, panel_count, GROUP, panel_rows), jnp.float32)],
        [place],
        parts,
    )
    whole = lax.all_to_all(split, "leaf", 0, 0, tiled=True)
    return whole.transpose(0, 2, 1, 3).reshape(rhs_rows, panel_count, panel_rows)


def replicates(rhs_rows, root_inverse):
    leaf_count, col_count = lax.axis_size("leaf"), lax.axis_size("col")
    panel_rows, own_columns = root_inverse.shape[1:]
    return (
        leaf_count == 8
        and col_count == 4
        and rhs_rows == GROUP * leaf_count
        and own_columns == 2 * panel_rows
    )


def local(
    right_sides,
    inverse_first,
    coupling_first,
    links_first,
    order_first,
    inverse_second,
    coupling_second,
    links_second,
    order_second,
    inverse_third,
    coupling_third,
    links_third,
    order_third,
    front_rows,
    root_inverse,
    root_coupling,
):
    level_data = (
        (inverse_first, coupling_first, links_first, order_first),
        (inverse_second, coupling_second, links_second, order_second),
        (inverse_third, coupling_third, links_third, order_third),
    )
    if replicates(right_sides.shape[0], root_inverse):
        place = jnp.stack([lax.axis_index("leaf"), lax.axis_index("col")]).astype(jnp.int32)
        solved, *sections = eliminate_all(place, right_sides, level_data, front_rows)
        return (*solved, root_replicated(place, *sections, root_inverse, root_coupling))
    section = right_sides
    outputs = []
    for level_index in range(3):
        inverse, coupling, link_ids, order_map = level_data[level_index]
        solved, skeleton = eliminate(
            section, inverse, coupling, link_ids, front_rows[level_index, 0]
        )
        outputs.append(solved)
        if level_index < 2:
            skeleton = join_halves(skeleton, level_index)
        skeleton = jnp.take(skeleton, order_map[0], axis=1)
        section = skeleton.reshape(skeleton.shape[0], -1)
    return (*outputs, root_wide(section, root_inverse, root_coupling))


def solution(mesh):
    in_specs = (
        P("col", "leaf"),
        P("leaf", None, None),
        P("leaf", None, None, None),
        P("leaf", None),
        P("leaf", None),
        P("leaf", None, None),
        P("leaf", None, None, None),
        P("leaf", None),
        P("leaf", None),
        P("leaf", None, None),
        P("leaf", None, None, None),
        P("leaf", None),
        P("leaf", None),
        P(None, "leaf"),
        P(None, "leaf", "col"),
        P("leaf", "col"),
    )
    out_specs = (P("col", "leaf"), P("col", "leaf"), P("col", "leaf"), P("col", None, "leaf"))
    return jax.shard_map(local, mesh=mesh, in_specs=in_specs, out_specs=out_specs, check_vma=False)
```

```python
import jax
import jax.numpy as jnp
from jax import lax
from jax.experimental import pallas as pl
from jax.experimental.pallas import tpu as pltpu
from jax.sharding import PartitionSpec as P


def partner(block, axis, stride):
    count = lax.axis_size(axis)
    route = []
    for low in range(count):
        high = low | 1 << stride
        if high != low and high < count:
            route += [(low, high), (high, low)]
    return lax.ppermute(block, axis, route)


def eliminate(section, inverse, coupling, link_ids, live_count):
    block_rows = inverse.shape[-1]
    red_blocks = inverse.shape[0]
    link_total = coupling.shape[1]
    rhs_rows = section.shape[0]
    skeleton_count = section.shape[1] // block_rows - red_blocks
    redundant = section[:, : red_blocks * block_rows].reshape(rhs_rows, red_blocks, block_rows)
    positions = lax.broadcasted_iota(
        jnp.int32, (red_blocks, block_rows), 0
    ) * block_rows + lax.broadcasted_iota(jnp.int32, (red_blocks, block_rows), 1)
    live_rows = (positions < live_count).astype(jnp.float32)
    solved = (
        jnp.einsum("rib,iba->ria", redundant * live_rows, inverse, precision=lax.Precision.HIGHEST)
        * live_rows
    )
    pushed = jnp.einsum("ria,ikab->rikb", solved, coupling, precision=lax.Precision.HIGHEST)
    targets = (
        link_ids[:, :, None]
        == lax.broadcasted_iota(jnp.int32, (red_blocks, link_total, skeleton_count), 2)
    ).astype(jnp.float32)
    update = jnp.einsum("rikb,iks->rsb", pushed, targets, precision=lax.Precision.HIGHEST)
    skeleton = (
        section[:, red_blocks * block_rows :].reshape(rhs_rows, skeleton_count, block_rows) - update
    )
    return (solved.reshape(rhs_rows, red_blocks * block_rows), skeleton)


def join_halves(skeleton, level_index):
    half_blocks = skeleton.shape[1] // 2
    upper_half = lax.axis_index("leaf") >> level_index & 1
    kept_half = lax.dynamic_slice_in_dim(skeleton, upper_half * half_blocks, half_blocks, 1)
    sent_half = lax.dynamic_slice_in_dim(skeleton, (1 - upper_half) * half_blocks, half_blocks, 1)
    received = partner(sent_half, "leaf", level_index)
    return jnp.where(
        upper_half == 0,
        jnp.concatenate([kept_half, received], 1),
        jnp.concatenate([received, kept_half], 1),
    )


def spread_columns(values):
    return lax.all_gather(values, "col", axis=0, tiled=True)


def spread_leaf(values):
    return lax.all_gather(values, "leaf", axis=0, tiled=True)


def to_leaf_rows(values):
    full_rows = lax.all_gather(values, "col", axis=1, tiled=True)
    return lax.all_to_all(full_rows, "leaf", split_axis=1, concat_axis=0, tiled=True)


def to_column_rows(values):
    full_rows = lax.all_gather(values, "leaf", axis=1, tiled=True)
    return lax.all_to_all(full_rows, "col", split_axis=1, concat_axis=0, tiled=True)


def forward_product(values, matrix):
    return lax.psum_scatter(
        jnp.dot(
            values, matrix, precision=lax.Precision.HIGHEST, preferred_element_type=jnp.float32
        ),
        "leaf",
        scatter_dimension=0,
        tiled=True,
    )


def backward_product(values, matrix):
    return lax.psum_scatter(
        lax.dot_general(
            values,
            matrix,
            (((1,), (1,)), ((), ())),
            precision=lax.Precision.HIGHEST,
            preferred_element_type=jnp.float32,
        ),
        "col",
        scatter_dimension=0,
        tiled=True,
    )


def root_wide(section, root_inverse, root_coupling):
    rhs_rows = section.shape[0]
    panel_count = root_inverse.shape[0]
    panel_rows = root_inverse.shape[1]
    root_rhs = section.reshape(rhs_rows, panel_count, panel_rows)
    full_rhs = spread_columns(root_rhs)
    first_solve = forward_product(full_rhs[:, 0], root_inverse[0])
    coupled = forward_product(to_leaf_rows(first_solve), root_coupling)
    second_solve = forward_product(full_rhs[:, 1] - to_leaf_rows(coupled), root_inverse[1])
    forward_both = spread_leaf(jnp.stack([first_solve, second_solve], 1))
    last_panel = backward_product(forward_both[:, 1], root_inverse[1])
    back_coupled = backward_product(to_column_rows(last_panel), root_coupling)
    first_panel = backward_product(
        forward_both[:, 0] - to_column_rows(back_coupled), root_inverse[0]
    )
    root_solution = jnp.stack([first_panel, last_panel], 1)
    return root_solution


GROUP = 8


def flip(block, axis, distance):
    count = lax.axis_size(axis)
    return lax.ppermute(block, axis, [(i, i ^ distance) for i in range(count)])


def swap_columns(parts):
    return [parts[0]] + [flip(parts[e], "col", e) for e in range(1, len(parts))]


def kernel_call(
    body, out_shapes, scalars, operands, loaded=(), ahead=(), stacks=(), held=(), scratch=(), room=40
):
    vmem = pl.BlockSpec(memory_space=pltpu.VMEM)
    far = pl.BlockSpec(memory_space=pltpu.HBM)
    out_shapes = [jax.ShapeDtypeStruct(shape, kind) for shape, kind in out_shapes]
    plain = len(out_shapes)
    out_shapes += [jax.ShapeDtypeStruct(value.shape, value.dtype) for value in ahead]
    moves, pieces = [], []
    for n, stack in enumerate(stacks):
        first = 0
        for piece in stack:
            piece, index = piece if isinstance(piece, tuple) else (piece, None)
            size = piece.shape[0] if index is None and piece.ndim == 3 else None
            moves.append((n, first, size, index))
            pieces.append(piece)
            first += size or 1
        out_shapes.append(jax.ShapeDtypeStruct((first, *pieces[-1].shape[-2:]), pieces[-1].dtype))
    loaded = [value if isinstance(value, tuple) else (value, None) for value in loaded]
    early = len(scalars) + len(loaded)
    inputs = (len(scalars), len(loaded), len(ahead), len(pieces), len(held), len(operands))
    counts = (*inputs, plain, len(ahead), len(stacks), early)
    waits = early + len(ahead) + 2 * len(pieces)

    def run(*refs):
        groups, start = [], 0
        for count in (*counts, len(refs)):
            groups.append(refs[start : start + count])
            start += count
        ints, loads, nexts, sources, _, ins, outs, next_outs, targets, fetched, rest = groups
        if waits:
            *rest, sems = rest
        loads = [ref if i is None else ref.at[i] for ref, (_, i) in zip(loads, loaded, strict=True)]
        pairs = list(zip((*ints, *loads, *nexts), (*fetched, *next_outs), strict=True))
        staged = list(rest[len(rest) - len(moves) :])
        rest = rest[: len(rest) - len(moves)]
        for source, stage, (_, _, _, index) in zip(sources, staged, moves, strict=True):
            pairs.append((source if index is None else source.at[index], stage))
        ends = [
            (stage, targets[n].at[first if size is None else pl.ds(first, size)])
            for stage, (n, first, size, _) in zip(staged, moves, strict=True)
        ]
        copies = [
            pltpu.make_async_copy(*pair, sems.at[n]) for n, pair in enumerate((*pairs, *ends))
        ]
        leaving = copies[len(pairs) :]
        for copy in copies[: len(pairs)]:
            copy.start()
        for copy in (*copies[:early], *copies[len(pairs) - len(moves) : len(pairs)]):
            copy.wait()
        for copy in leaving:
            copy.start()
        place = (lax.axis_index("leaf"), lax.axis_index("col"))
        body(place, *fetched, *ins, *outs, *rest)
        for copy in (*copies[early : len(pairs) - len(moves)], *leaving):
            copy.wait()

    fetched = [pltpu.SMEM(value.shape, value.dtype) for value in scalars]
    fetched += [pltpu.VMEM(value.shape[i is not None :], value.dtype) for value, i in loaded]
    stages = [
        pltpu.VMEM(piece.shape[index is not None :], piece.dtype)
        for piece, (_, _, _, index) in zip(pieces, moves, strict=True)
    ]
    sems = [pltpu.SemaphoreType.DMA((waits,))] if waits else []
    return pl.pallas_call(
        run,
        out_shape=out_shapes,
        in_specs=[far] * sum(inputs[:-2])
        + [pl.BlockSpec(memory_space=pl.ANY)] * len(held)
        + [vmem] * len(operands),
        out_specs=[vmem] * (plain + len(ahead)) + [far] * len(stacks),
        scratch_shapes=fetched + list(scratch) + stages + sems,
        compiler_params=pltpu.CompilerParams(vmem_limit_bytes=room * 1024 * 1024),
    )(*scalars, *[value for value, _ in loaded], *ahead, *pieces, *held, *operands)


def halves(values):
    high = values.astype(jnp.bfloat16)
    return high, (values - high.astype(jnp.float32)).astype(jnp.bfloat16)


def product(values, high, low, contract):
    rows = values.shape[0]
    own_high, own_low = halves(values)
    dims = (((1,), (contract,)), ((), ()))
    both = lax.dot_general(
        jnp.concatenate([own_high, own_low], 0), high, dims, preferred_element_type=jnp.float32
    )
    cross = lax.dot_general(own_high, low, dims, preferred_element_type=jnp.float32)
    return both[:rows] + both[rows:] + cross


def regroup(values, distance, parts):
    if distance == 0:
        return values
    size = values.shape[0] // parts
    return jnp.concatenate(
        [values[(d ^ distance) * size : (d ^ distance) * size + size] for d in range(parts)], 0
    )


def span(index, size):
    return pl.ds(pl.multiple_of(index * size, size), size)


def gate(values, after):
    far = pl.BlockSpec(memory_space=pltpu.HBM)

    def run(*refs):
        pass

    return pl.pallas_call(
        run,
        out_shape=[jax.ShapeDtypeStruct(value.shape, value.dtype) for value in values],
        in_specs=[far] * len(values) + [pl.BlockSpec(memory_space=pltpu.VMEM)] * len(after),
        out_specs=[far] * len(values),
        input_output_aliases={n: n for n in range(len(values))},
        compiler_params=pltpu.CompilerParams(vmem_limit_bytes=1024 * 1024),
    )(*values, *after)


def join_kernel(place, kept, received, joined):
    half = kept.shape[1] // 2
    joined[:, :half] = kept[:, :half]
    joined[:, half:] = received[:, :half]


def assemble_kernel(place, *refs):
    *blocks, high, low = refs
    rows = blocks[0].shape[0]
    for n, block in enumerate(blocks):
        core, chip = divmod(n, len(blocks) // 2)
        where = span(place[0] ^ core ^ 2 * chip, rows)
        high[where, :], low[where, :] = halves(block[...])


def assemble(parts):
    rows, width = parts[0][0].shape[-2:]
    panel = ((rows * lax.axis_size("leaf"), width), jnp.bfloat16)
    return kernel_call(assemble_kernel, [panel, panel], [], [], loaded=parts)


def pair_kernel(place, own, other, high, low):
    rows = own.shape[0]
    high[:rows, :], low[:rows, :] = halves(own[...])
    high[rows:, :], low[rows:, :] = halves(other[...])


def first_kernel(place, *refs):
    count = (len(refs) - 5) // 2
    parts, (high, low, kept, received) = refs[:count], refs[count : count + 4]
    sent, pushed = refs[count + 4 : -1], refs[-1]
    rows, width = parts[0].shape
    values = product(jnp.concatenate([part[...] for part in parts], 0), high[...], low[...], 0)
    for e in range(count):
        pushed[e] = values[e * rows : (e + 1) * rows]
    chip, lower = place[0] >> 1, (place[0] & 1) == 0
    half = width // 2
    for f, part in enumerate(sent):
        where = span(chip ^ f, GROUP)
        for e in range(count):
            part[e * GROUP : (e + 1) * GROUP, :] = pushed[e, where, :]
        own, other = kept[where, half:], received[where, half:]
        part[rows:, :half] = jnp.where(lower, own, other)
        part[rows:, half:] = jnp.where(lower, other, own)


def share_kernel(place, *refs):
    count = (len(refs) - 1) // 2
    parts, sent, rest = refs[:count], refs[count:-1], refs[-1]
    rows = parts[0].shape[0] - GROUP
    total = sum(part[:rows, :] for part in parts[1:]) + parts[0][:rows, :]
    for f, part in enumerate(parts):
        rest[f] = part[rows:, :]
    for e, part in enumerate(sent):
        part[:rows, :] = total
        part[rows:, :] = rest[(place[0] >> 1) ^ place[1] ^ e]


def gathered_product(place, parts, high, low):
    count = len(parts)
    width = parts[0].shape[1]
    total = None
    for e, part in enumerate(parts):
        rows = span(place[1] ^ e, width)
        values = part[: count * GROUP, :]
        term = product(regroup(values, e, count), high[rows, :], low[rows, :], 0)
        total = term if total is None else total + term
    return total


def coupled_kernel(place, *refs):
    parts, (high, low, result) = refs[:-3], refs[-3:]
    rest = jnp.concatenate([part[len(parts) * GROUP :, :] for part in parts], 0)
    result[...] = rest - gathered_product(place, parts, high, low)


def scatter_product(place, values, high, low, sent):
    count = len(sent)
    width = sent[0].shape[1]
    for e, part in enumerate(sent):
        rows = span(place[1] ^ e, width)
        part[...] = regroup(product(values, high[rows, :], low[rows, :], 1), e, count)


def turn_kernel(place, *refs):
    count = (len(refs) - 2) // 2
    parts, (high, low), sent = refs[:count], refs[count : count + 2], refs[count + 2 :]
    second = gathered_product(place, parts, high, low)
    scatter_product(place, second, high, low, sent)


def back_kernel(place, *refs):
    count = (len(refs) - 2) // 2
    parts, (high, low), sent = refs[:count], refs[count : count + 2], refs[count + 2 :]
    total = sum(part[...] for part in parts[1:]) + parts[0][...]
    rows, width = total.shape
    for e, part in enumerate(sent):
        where = span(place[1] ^ e, width)
        value = product(total, high[where, :], low[where, :], 1)
        part[:rows, :] = regroup(value, e, count)
        part[rows:, :] = total[e * GROUP : (e + 1) * GROUP]


def spread_kernel(place, *refs):
    count = (len(refs) - 2) // 2
    parts, first, sent, rest = refs[:count], refs[count], refs[count + 1 : -1], refs[-1]
    rows = parts[0].shape[0] - GROUP
    total = sum(part[:rows, :] for part in parts[1:]) + parts[0][:rows, :]
    for e, part in enumerate(parts):
        rest[e] = part[rows:, :]
    for f, part in enumerate(sent):
        part[:rows, :] = first[:rows, :] - total
        part[rows:, :] = rest[(place[0] >> 1) ^ place[1] ^ f]


def last_kernel(place, *refs):
    count = (len(refs) - 4) // 2
    parts, (high, low), last, sent, joined = (
        refs[:count],
        refs[count : count + 2],
        refs[-2],
        refs[count + 2 : -2],
        refs[-1],
    )
    rows = parts[0].shape[0] - GROUP
    chip = place[0] >> 1
    for f, part in enumerate(parts):
        for e in range(count):
            joined[e, span(chip ^ f, GROUP), :] = part[e * GROUP : (e + 1) * GROUP, :]
        last[span(chip ^ f, GROUP), :] = part[rows:, :]
    values = jnp.concatenate([joined[e] for e in range(count)], 0)
    values = product(values, high[...], low[...], 1)
    for e, part in enumerate(sent):
        part[...] = values[e * rows : (e + 1) * rows]


def part_kernel(place, *refs):
    parts, (last, kept, sent) = refs[:-3], refs[-3:]
    total = sum(part[...] for part in parts[1:]) + parts[0][...]
    half = total.shape[1] // 2
    lower = (place[0] & 1) == 0
    for n, panel in enumerate((total, last[...])):
        own, other = panel[:, :half], panel[:, half:]
        if n:
            own, other = jnp.where(lower, own, other), jnp.where(lower, other, own)
        kept[:, n * half : (n + 1) * half] = own
        sent[:, n * half : (n + 1) * half] = other


def merge_kernel(place, kept, received, result):
    panels, half = result.shape[1:]
    lower = (place[0] & 1) == 0
    for chip in range(kept.shape[0] // GROUP):
        rows = slice(chip * GROUP, (chip + 1) * GROUP)
        for n in range(panels):
            columns = slice(n * half, (n + 1) * half)
            own, other = kept[rows, columns], received[rows, columns]
            start = 2 * chip * GROUP
            result[start : start + GROUP, n, :] = jnp.where(lower, own, other)
            result[start + GROUP : start + 2 * GROUP, n, :] = jnp.where(lower, other, own)


def reduce_blocks(level, live, links, blocks, inverse, coupling, solved):
    red_blocks, link_total, size = inverse.shape[0], coupling.shape[1], inverse.shape[1]
    lanes = lax.broadcasted_iota(jnp.int32, (1, size), 1)
    pushed = []
    for i in range(red_blocks):
        mask = (lanes + i * size < live[0, level]).astype(jnp.float32)
        value = product(blocks[i] * mask, *halves(inverse[i]), 0) * mask
        solved[:, i * size : (i + 1) * size] = value
        pairs = [halves(coupling[i, k]) for k in range(link_total)]
        high, low = (jnp.concatenate(part, 1) for part in zip(*pairs, strict=True))
        pushed.append(product(value, high, low, 0))
    for i in range(red_blocks):
        for k in range(link_total):
            target = red_blocks + links[i, k]
            blocks[target] = blocks[target] - pushed[i][:, k * size : (k + 1) * size]


def send_halves(place, level, blocks, red_blocks, kept, sent):
    half = kept.shape[0]
    upper = (place[0] >> level) & 1
    kept[...] = blocks[pl.ds(red_blocks + upper * half, half)]
    sent[...] = blocks[pl.ds(red_blocks + (1 - upper) * half, half)]


def load_halves(place, level, order, kept, received, joined, blocks):
    half = kept.shape[0]
    upper = (place[0] >> level) & 1
    joined[pl.ds(upper * half, half)] = kept[...]
    joined[pl.ds((1 - upper) * half, half)] = received[...]
    for n in range(2 * half):
        blocks[n] = joined[order[0, n]]


def lowest_kernel(place, live, links, section, inverse, coupling, solved, kept, sent, blocks):
    size = inverse.shape[1]
    for n in range(blocks.shape[0]):
        blocks[n] = section[:, n * size : (n + 1) * size]
    reduce_blocks(0, live, links, blocks, inverse, coupling, solved)
    send_halves(place, 0, blocks, inverse.shape[0], kept, sent)


def middle_kernel(
    place, live, links, order, old, received, inverse, coupling, solved, kept, sent, joined, blocks
):
    load_halves(place, 0, order, old, received, joined, blocks)
    reduce_blocks(1, live, links, blocks, inverse, coupling, solved)
    send_halves(place, 1, blocks, inverse.shape[0], kept, sent)


def highest_kernel(
    place, live, links, order, last_order, old, received, inverse, coupling, solved, kept, sent, joined, blocks
):
    load_halves(place, 1, order, old, received, joined, blocks)
    reduce_blocks(2, live, links, blocks, inverse, coupling, solved)
    red_blocks, size = inverse.shape[0], inverse.shape[1]
    core = place[0] & 1
    for n in range(blocks.shape[0] - red_blocks):
        block = red_blocks + last_order[0, n]
        columns = slice(n * size, (n + 1) * size)
        for chip in range(kept.shape[0] // GROUP):
            rows = slice(chip * GROUP, (chip + 1) * GROUP)
            kept[rows, columns] = blocks[block, span(2 * chip + core, GROUP), :]
            sent[rows, columns] = blocks[block, span(2 * chip + 1 - core, GROUP), :]


def swap_chips(parts):
    return [parts[0]] + [flip(parts[f], "leaf", 2 * f) for f in range(1, len(parts))]


def solve_tree(right_sides, level_data, front_rows, root_inverse, root_coupling):
    leaf_count, col_count = lax.axis_size("leaf"), lax.axis_size("col")
    chip_count = leaf_count // 2
    panel_count, panel_rows, own_columns = root_inverse.shape
    group = GROUP * col_count
    rhs_rows = right_sides.shape[0]
    front_rows = front_rows.reshape(1, -1)
    red_blocks, size = level_data[0][0].shape[:2]
    solved = ((rhs_rows, red_blocks * size), jnp.float32)
    pair = ((2 * panel_rows, own_columns), jnp.bfloat16)
    one = ((group, own_columns), jnp.float32)
    more = ((group + GROUP, own_columns), jnp.float32)
    both = ((group, panel_count * panel_rows), jnp.float32)

    def halved(count):
        return (((count - red_blocks) // 2, rhs_rows, size), jnp.float32)

    def scratch(*shape):
        return pltpu.VMEM(shape, jnp.float32)

    inverse, coupling, links, order = level_data[0]
    count = right_sides.shape[1] // size
    solved_first, kept, sent, second = kernel_call(
        lowest_kernel,
        [solved, halved(count), halved(count)],
        [front_rows, links],
        [],
        loaded=[right_sides, inverse, coupling],
        stacks=[[(root_inverse, 1)]],
        scratch=[scratch(count, rhs_rows, size)],
        room=64,
    )
    received = flip(sent, "leaf", 1)
    far = flip(root_coupling, "leaf", 4)
    second_far = flip(second, "leaf", 4)
    near = flip(root_coupling, "leaf", 2)
    partner_inverse = flip(root_inverse, "leaf", 1)
    partner_coupling = flip(root_coupling, "leaf", 1)
    inverse, coupling, links, next_order = level_data[1]
    count -= red_blocks
    solved_second, kept, sent = kernel_call(
        middle_kernel,
        [solved, halved(count), halved(count)],
        [front_rows, links, order],
        [kept, received, inverse, coupling],
        held=[partner_inverse, partner_coupling],
        scratch=[scratch(count, rhs_rows, size)] * 2,
        room=64,
    )
    received = flip(sent, "leaf", 2)
    inverse, coupling, links, last_order = level_data[2]
    count -= red_blocks
    solved_third, kept, sent, near, second = kernel_call(
        highest_kernel,
        [solved, both, both],
        [front_rows, links, next_order, last_order],
        [kept, received, inverse, coupling],
        stacks=[[near], [(root_inverse, 1)]],
        held=[far],
        scratch=[scratch(count, rhs_rows, size)] * 2,
        room=64,
    )
    received = flip(sent, "leaf", 1)
    corner = flip(near, "leaf", 4)
    second_near = flip(second, "leaf", 2)
    partner_near = flip(near, "leaf", 1)
    (joined,) = kernel_call(join_kernel, [both], [], [kept, received], held=[partner_near, second_far])

    near_high, near_low = kernel_call(pair_kernel, [pair, pair], [], [], loaded=[(root_inverse, 0), (partner_inverse, 0)])
    parts = swap_columns([joined] * col_count)
    parts = kernel_call(
        first_kernel,
        [more] * chip_count,
        [],
        [*parts, near_high, near_low, kept, received],
        held=[corner, second_near],
        scratch=[scratch(col_count, group, own_columns)],
    )
    corner, far = gate([corner, far], [parts[-1]])
    partner_corner = flip(corner, "leaf", 1)
    partner_far = flip(far, "leaf", 1)
    parts = kernel_call(
        share_kernel,
        [more] * col_count,
        [],
        swap_chips(parts),
        held=[partner_far, partner_corner],
        scratch=[scratch(chip_count, GROUP, own_columns)],
    )
    (second_far,) = gate([second_far], [parts[-1]])
    second_corner = flip(second_far, "leaf", 2)
    partner_second = flip(second_far, "leaf", 1)
    between = assemble(
        [(root_coupling, None), (near, 0), (far, None), (corner, 0)]
        + [(partner_coupling, None), (partner_near, 0), (partner_far, None), (partner_corner, 0)]
    )
    first_sum = parts[0]
    parts = swap_columns(parts)
    (left,) = kernel_call(coupled_kernel, [one], [], [*parts, *between])
    second_near, second_corner = gate([second_near, second_corner], [left])
    panel = assemble(
        [(root_inverse, 1), (second_near, 0), (second_far, 0), (second_corner, 0)]
        + [(partner_inverse, 1), (flip(second_near, "leaf", 1), 0)]
        + [(partner_second, 0), (flip(second_corner, "leaf", 1), 0)]
    )
    parts = swap_columns([left] * col_count)
    parts = kernel_call(turn_kernel, [one] * col_count, [], [*parts, *panel])
    parts = swap_columns(parts)
    parts = kernel_call(back_kernel, [more] * col_count, [], [*parts, *between])
    parts = swap_columns(parts)
    parts = kernel_call(
        spread_kernel,
        [more] * chip_count,
        [],
        [*parts, first_sum],
        scratch=[scratch(col_count, GROUP, own_columns)],
    )
    *parts, last = kernel_call(
        last_kernel,
        [one] * (col_count + 1),
        [],
        [*swap_chips(parts), near_high, near_low],
        scratch=[scratch(col_count, group, own_columns)],
    )
    kept, sent = kernel_call(part_kernel, [both, both], [], [*swap_columns(parts), last])
    (result,) = kernel_call(
        merge_kernel,
        [((rhs_rows, panel_count, panel_rows), jnp.float32)],
        [],
        [kept, flip(sent, "leaf", 1)],
    )
    return (solved_first, solved_second, solved_third, result)


def replicates(rhs_rows, root_inverse):
    leaf_count, col_count = lax.axis_size("leaf"), lax.axis_size("col")
    panel_rows, own_columns = root_inverse.shape[1:]
    return (
        leaf_count == 8
        and col_count == 4
        and rhs_rows == GROUP * leaf_count
        and own_columns == 2 * panel_rows
    )


def local(
    right_sides,
    inverse_first,
    coupling_first,
    links_first,
    order_first,
    inverse_second,
    coupling_second,
    links_second,
    order_second,
    inverse_third,
    coupling_third,
    links_third,
    order_third,
    front_rows,
    root_inverse,
    root_coupling,
):
    level_data = (
        (inverse_first, coupling_first, links_first, order_first),
        (inverse_second, coupling_second, links_second, order_second),
        (inverse_third, coupling_third, links_third, order_third),
    )
    if replicates(right_sides.shape[0], root_inverse):
        return solve_tree(right_sides, level_data, front_rows, root_inverse, root_coupling)
    section = right_sides
    outputs = []
    for level_index in range(3):
        inverse, coupling, link_ids, order_map = level_data[level_index]
        solved, skeleton = eliminate(
            section, inverse, coupling, link_ids, front_rows[level_index, 0]
        )
        outputs.append(solved)
        if level_index < 2:
            skeleton = join_halves(skeleton, level_index)
        skeleton = jnp.take(skeleton, order_map[0], axis=1)
        section = skeleton.reshape(skeleton.shape[0], -1)
    return (*outputs, root_wide(section, root_inverse, root_coupling))


def solution(mesh):
    in_specs = (
        P("col", "leaf"),
        P("leaf", None, None),
        P("leaf", None, None, None),
        P("leaf", None),
        P("leaf", None),
        P("leaf", None, None),
        P("leaf", None, None, None),
        P("leaf", None),
        P("leaf", None),
        P("leaf", None, None),
        P("leaf", None, None, None),
        P("leaf", None),
        P("leaf", None),
        P(None, "leaf"),
        P(None, "leaf", "col"),
        P("leaf", "col"),
    )
    out_specs = (P("col", "leaf"), P("col", "leaf"), P("col", "leaf"), P("col", None, "leaf"))
    return jax.shard_map(local, mesh=mesh, in_specs=in_specs, out_specs=out_specs, check_vma=False)
```

```python
import jax
import jax.numpy as jnp
from jax import lax
from jax.experimental import pallas as pl
from jax.experimental.pallas import tpu as pltpu
from jax.sharding import PartitionSpec as P


def partner(block, axis, stride):
    count = lax.axis_size(axis)
    route = []
    for low in range(count):
        high = low | 1 << stride
        if high != low and high < count:
            route += [(low, high), (high, low)]
    return lax.ppermute(block, axis, route)


def eliminate(section, inverse, coupling, link_ids, live_count):
    block_rows = inverse.shape[-1]
    red_blocks = inverse.shape[0]
    link_total = coupling.shape[1]
    rhs_rows = section.shape[0]
    skeleton_count = section.shape[1] // block_rows - red_blocks
    redundant = section[:, : red_blocks * block_rows].reshape(rhs_rows, red_blocks, block_rows)
    positions = lax.broadcasted_iota(
        jnp.int32, (red_blocks, block_rows), 0
    ) * block_rows + lax.broadcasted_iota(jnp.int32, (red_blocks, block_rows), 1)
    live_rows = (positions < live_count).astype(jnp.float32)
    solved = (
        jnp.einsum("rib,iba->ria", redundant * live_rows, inverse, precision=lax.Precision.HIGHEST)
        * live_rows
    )
    pushed = jnp.einsum("ria,ikab->rikb", solved, coupling, precision=lax.Precision.HIGHEST)
    targets = (
        link_ids[:, :, None]
        == lax.broadcasted_iota(jnp.int32, (red_blocks, link_total, skeleton_count), 2)
    ).astype(jnp.float32)
    update = jnp.einsum("rikb,iks->rsb", pushed, targets, precision=lax.Precision.HIGHEST)
    skeleton = (
        section[:, red_blocks * block_rows :].reshape(rhs_rows, skeleton_count, block_rows) - update
    )
    return (solved.reshape(rhs_rows, red_blocks * block_rows), skeleton)


def join_halves(skeleton, level_index):
    half_blocks = skeleton.shape[1] // 2
    upper_half = lax.axis_index("leaf") >> level_index & 1
    kept_half = lax.dynamic_slice_in_dim(skeleton, upper_half * half_blocks, half_blocks, 1)
    sent_half = lax.dynamic_slice_in_dim(skeleton, (1 - upper_half) * half_blocks, half_blocks, 1)
    received = partner(sent_half, "leaf", level_index)
    return jnp.where(
        upper_half == 0,
        jnp.concatenate([kept_half, received], 1),
        jnp.concatenate([received, kept_half], 1),
    )


def spread_columns(values):
    return lax.all_gather(values, "col", axis=0, tiled=True)


def spread_leaf(values):
    return lax.all_gather(values, "leaf", axis=0, tiled=True)


def to_leaf_rows(values):
    full_rows = lax.all_gather(values, "col", axis=1, tiled=True)
    return lax.all_to_all(full_rows, "leaf", split_axis=1, concat_axis=0, tiled=True)


def to_column_rows(values):
    full_rows = lax.all_gather(values, "leaf", axis=1, tiled=True)
    return lax.all_to_all(full_rows, "col", split_axis=1, concat_axis=0, tiled=True)


def forward_product(values, matrix):
    return lax.psum_scatter(
        jnp.dot(
            values, matrix, precision=lax.Precision.HIGHEST, preferred_element_type=jnp.float32
        ),
        "leaf",
        scatter_dimension=0,
        tiled=True,
    )


def backward_product(values, matrix):
    return lax.psum_scatter(
        lax.dot_general(
            values,
            matrix,
            (((1,), (1,)), ((), ())),
            precision=lax.Precision.HIGHEST,
            preferred_element_type=jnp.float32,
        ),
        "col",
        scatter_dimension=0,
        tiled=True,
    )


def root_wide(section, root_inverse, root_coupling):
    rhs_rows = section.shape[0]
    panel_count = root_inverse.shape[0]
    panel_rows = root_inverse.shape[1]
    root_rhs = section.reshape(rhs_rows, panel_count, panel_rows)
    full_rhs = spread_columns(root_rhs)
    first_solve = forward_product(full_rhs[:, 0], root_inverse[0])
    coupled = forward_product(to_leaf_rows(first_solve), root_coupling)
    second_solve = forward_product(full_rhs[:, 1] - to_leaf_rows(coupled), root_inverse[1])
    forward_both = spread_leaf(jnp.stack([first_solve, second_solve], 1))
    last_panel = backward_product(forward_both[:, 1], root_inverse[1])
    back_coupled = backward_product(to_column_rows(last_panel), root_coupling)
    first_panel = backward_product(
        forward_both[:, 0] - to_column_rows(back_coupled), root_inverse[0]
    )
    root_solution = jnp.stack([first_panel, last_panel], 1)
    return root_solution


GROUP = 8


def flip(block, axis, distance):
    count = lax.axis_size(axis)
    return lax.ppermute(block, axis, [(i, i ^ distance) for i in range(count)])


def swap_columns(parts):
    return [parts[0]] + [flip(parts[e], "col", e) for e in range(1, len(parts))]


def kernel_call(
    body, out_shapes, scalars, operands, loaded=(), ahead=(), stacks=(), held=(), scratch=(), room=40, late=0
):
    vmem = pl.BlockSpec(memory_space=pltpu.VMEM)
    far = pl.BlockSpec(memory_space=pltpu.HBM)
    out_shapes = [jax.ShapeDtypeStruct(shape, kind) for shape, kind in out_shapes]
    plain = len(out_shapes)
    out_shapes += [jax.ShapeDtypeStruct(value.shape, value.dtype) for value in ahead]
    moves, pieces = [], []
    for n, stack in enumerate(stacks):
        first = 0
        for piece in stack:
            piece, index = piece if isinstance(piece, tuple) else (piece, None)
            size = piece.shape[0] if index is None and piece.ndim == 3 else None
            moves.append((n, first, size, index))
            pieces.append(piece)
            first += size or 1
        out_shapes.append(jax.ShapeDtypeStruct((first, *pieces[-1].shape[-2:]), pieces[-1].dtype))
    loaded = [value if isinstance(value, tuple) else (value, None) for value in loaded]
    early = len(scalars) + len(loaded)
    inputs = (len(scalars), len(loaded), len(ahead), len(pieces), len(held), len(operands))
    counts = (*inputs, plain, len(ahead), len(stacks), early)
    waits = early + len(ahead) + 2 * len(pieces)

    def run(*refs):
        groups, start = [], 0
        for count in (*counts, len(refs)):
            groups.append(refs[start : start + count])
            start += count
        ints, loads, nexts, sources, _, ins, outs, next_outs, targets, fetched, rest = groups
        if waits:
            *rest, sems = rest
        loads = [ref if i is None else ref.at[i] for ref, (_, i) in zip(loads, loaded, strict=True)]
        pairs = list(zip((*ints, *loads, *nexts), (*fetched, *next_outs), strict=True))
        staged = list(rest[len(rest) - len(moves) :])
        rest = rest[: len(rest) - len(moves)]
        for source, stage, (_, _, _, index) in zip(sources, staged, moves, strict=True):
            pairs.append((source if index is None else source.at[index], stage))
        ends = [
            (stage, targets[n].at[first if size is None else pl.ds(first, size)])
            for stage, (n, first, size, _) in zip(staged, moves, strict=True)
        ]
        copies = [
            pltpu.make_async_copy(*pair, sems.at[n]) for n, pair in enumerate((*pairs, *ends))
        ]
        leaving = copies[len(pairs) :]
        for copy in copies[: len(pairs)]:
            copy.start()
        for copy in copies[: early - late]:
            copy.wait()

        def ready():
            for copy in (*copies[early - late : early], *copies[len(pairs) - len(moves) : len(pairs)]):
                copy.wait()
            for copy in leaving:
                copy.start()

        place = (lax.axis_index("leaf"), lax.axis_index("col"), ready)
        if not late:
            ready()
        body(place, *fetched, *ins, *outs, *rest)
        for copy in (*copies[early : len(pairs) - len(moves)], *leaving):
            copy.wait()

    fetched = [pltpu.SMEM(value.shape, value.dtype) for value in scalars]
    fetched += [pltpu.VMEM(value.shape[i is not None :], value.dtype) for value, i in loaded]
    stages = [
        pltpu.VMEM(piece.shape[index is not None :], piece.dtype)
        for piece, (_, _, _, index) in zip(pieces, moves, strict=True)
    ]
    sems = [pltpu.SemaphoreType.DMA((waits,))] if waits else []
    return pl.pallas_call(
        run,
        out_shape=out_shapes,
        in_specs=[far] * sum(inputs[:-2])
        + [pl.BlockSpec(memory_space=pl.ANY)] * len(held)
        + [vmem] * len(operands),
        out_specs=[vmem] * (plain + len(ahead)) + [far] * len(stacks),
        scratch_shapes=fetched + list(scratch) + stages + sems,
        compiler_params=pltpu.CompilerParams(vmem_limit_bytes=room * 1024 * 1024),
    )(*scalars, *[value for value, _ in loaded], *ahead, *pieces, *held, *operands)


def halves(values):
    high = values.astype(jnp.bfloat16)
    return high, (values - high.astype(jnp.float32)).astype(jnp.bfloat16)


def product(values, high, low, contract):
    rows = values.shape[0]
    own_high, own_low = halves(values)
    dims = (((1,), (contract,)), ((), ()))
    both = lax.dot_general(
        jnp.concatenate([own_high, own_low], 0), high, dims, preferred_element_type=jnp.float32
    )
    cross = lax.dot_general(own_high, low, dims, preferred_element_type=jnp.float32)
    return both[:rows] + both[rows:] + cross


def regroup(values, distance, parts):
    if distance == 0:
        return values
    size = values.shape[0] // parts
    return jnp.concatenate(
        [values[(d ^ distance) * size : (d ^ distance) * size + size] for d in range(parts)], 0
    )


def span(index, size):
    return pl.ds(pl.multiple_of(index * size, size), size)


def gate(values, after):
    far = pl.BlockSpec(memory_space=pltpu.HBM)

    def run(*refs):
        pass

    return pl.pallas_call(
        run,
        out_shape=[jax.ShapeDtypeStruct(value.shape, value.dtype) for value in values],
        in_specs=[far] * len(values) + [pl.BlockSpec(memory_space=pltpu.VMEM)] * len(after),
        out_specs=[far] * len(values),
        input_output_aliases={n: n for n in range(len(values))},
        compiler_params=pltpu.CompilerParams(vmem_limit_bytes=1024 * 1024),
    )(*values, *after)


def join_kernel(place, kept, received, joined):
    half = kept.shape[1] // 2
    joined[:, :half] = kept[:, :half]
    joined[:, half:] = received[:, :half]


def assemble_kernel(place, *refs):
    *blocks, high, low = refs
    rows = blocks[0].shape[0]
    for n, block in enumerate(blocks):
        core, chip = divmod(n, len(blocks) // 2)
        where = span(place[0] ^ core ^ 2 * chip, rows)
        high[where, :], low[where, :] = halves(block[...])


def assemble(parts):
    rows, width = parts[0][0].shape[-2:]
    panel = ((rows * lax.axis_size("leaf"), width), jnp.bfloat16)
    return kernel_call(assemble_kernel, [panel, panel], [], [], loaded=parts)


def pair_kernel(place, own, other, high, low):
    rows = own.shape[0]
    high[:rows, :], low[:rows, :] = halves(own[...])
    high[rows:, :], low[rows:, :] = halves(other[...])


def first_kernel(place, *refs):
    count = (len(refs) - 5) // 2
    parts, (high, low, kept, received) = refs[:count], refs[count : count + 4]
    sent, pushed = refs[count + 4 : -1], refs[-1]
    rows, width = parts[0].shape
    values = product(jnp.concatenate([part[...] for part in parts], 0), high[...], low[...], 0)
    for e in range(count):
        pushed[e] = values[e * rows : (e + 1) * rows]
    chip, lower = place[0] >> 1, (place[0] & 1) == 0
    half = width // 2
    for f, part in enumerate(sent):
        where = span(chip ^ f, GROUP)
        for e in range(count):
            part[e * GROUP : (e + 1) * GROUP, :] = pushed[e, where, :]
        own, other = kept[where, half:], received[where, half:]
        part[rows:, :half] = jnp.where(lower, own, other)
        part[rows:, half:] = jnp.where(lower, other, own)


def share_kernel(place, *refs):
    count = (len(refs) - 1) // 2
    parts, sent, rest = refs[:count], refs[count:-1], refs[-1]
    rows = parts[0].shape[0] - GROUP
    total = sum(part[:rows, :] for part in parts[1:]) + parts[0][:rows, :]
    for f, part in enumerate(parts):
        rest[f] = part[rows:, :]
    for e, part in enumerate(sent):
        part[:rows, :] = total
        part[rows:, :] = rest[(place[0] >> 1) ^ place[1] ^ e]


def gathered_product(place, parts, high, low):
    count = len(parts)
    width = parts[0].shape[1]
    total = None
    for e, part in enumerate(parts):
        rows = span(place[1] ^ e, width)
        values = part[: count * GROUP, :]
        term = product(regroup(values, e, count), high[rows, :], low[rows, :], 0)
        total = term if total is None else total + term
    return total


def coupled_kernel(place, *refs):
    parts, (high, low, result) = refs[:-3], refs[-3:]
    rest = jnp.concatenate([part[len(parts) * GROUP :, :] for part in parts], 0)
    result[...] = rest - gathered_product(place, parts, high, low)


def scatter_product(place, values, high, low, sent):
    count = len(sent)
    width = sent[0].shape[1]
    for e, part in enumerate(sent):
        rows = span(place[1] ^ e, width)
        part[...] = regroup(product(values, high[rows, :], low[rows, :], 1), e, count)


def turn_kernel(place, *refs):
    count = (len(refs) - 2) // 2
    parts, (high, low), sent = refs[:count], refs[count : count + 2], refs[count + 2 :]
    second = gathered_product(place, parts, high, low)
    scatter_product(place, second, high, low, sent)


def back_kernel(place, *refs):
    count = (len(refs) - 2) // 2
    parts, (high, low), sent = refs[:count], refs[count : count + 2], refs[count + 2 :]
    total = sum(part[...] for part in parts[1:]) + parts[0][...]
    rows, width = total.shape
    for e, part in enumerate(sent):
        where = span(place[1] ^ e, width)
        value = product(total, high[where, :], low[where, :], 1)
        part[:rows, :] = regroup(value, e, count)
        part[rows:, :] = total[e * GROUP : (e + 1) * GROUP]


def spread_kernel(place, *refs):
    count = (len(refs) - 2) // 2
    parts, first, sent, rest = refs[:count], refs[count], refs[count + 1 : -1], refs[-1]
    rows = parts[0].shape[0] - GROUP
    total = sum(part[:rows, :] for part in parts[1:]) + parts[0][:rows, :]
    for e, part in enumerate(parts):
        rest[e] = part[rows:, :]
    for f, part in enumerate(sent):
        part[:rows, :] = first[:rows, :] - total
        part[rows:, :] = rest[(place[0] >> 1) ^ place[1] ^ f]


def last_kernel(place, *refs):
    count = (len(refs) - 4) // 2
    parts, (high, low), last, sent, joined = (
        refs[:count],
        refs[count : count + 2],
        refs[-2],
        refs[count + 2 : -2],
        refs[-1],
    )
    rows = parts[0].shape[0] - GROUP
    chip = place[0] >> 1
    for f, part in enumerate(parts):
        for e in range(count):
            joined[e, span(chip ^ f, GROUP), :] = part[e * GROUP : (e + 1) * GROUP, :]
        last[span(chip ^ f, GROUP), :] = part[rows:, :]
    values = jnp.concatenate([joined[e] for e in range(count)], 0)
    values = product(values, high[...], low[...], 1)
    for e, part in enumerate(sent):
        part[...] = values[e * rows : (e + 1) * rows]


def part_kernel(place, *refs):
    parts, (last, kept, sent) = refs[:-3], refs[-3:]
    total = sum(part[...] for part in parts[1:]) + parts[0][...]
    half = total.shape[1] // 2
    lower = (place[0] & 1) == 0
    for n, panel in enumerate((total, last[...])):
        own, other = panel[:, :half], panel[:, half:]
        if n:
            own, other = jnp.where(lower, own, other), jnp.where(lower, other, own)
        kept[:, n * half : (n + 1) * half] = own
        sent[:, n * half : (n + 1) * half] = other


def merge_kernel(place, kept, received, result):
    panels, half = result.shape[1:]
    lower = (place[0] & 1) == 0
    for chip in range(kept.shape[0] // GROUP):
        rows = slice(chip * GROUP, (chip + 1) * GROUP)
        for n in range(panels):
            columns = slice(n * half, (n + 1) * half)
            own, other = kept[rows, columns], received[rows, columns]
            start = 2 * chip * GROUP
            result[start : start + GROUP, n, :] = jnp.where(lower, own, other)
            result[start + GROUP : start + 2 * GROUP, n, :] = jnp.where(lower, other, own)


def reduce_blocks(ready, level, live, links, blocks, inverse, coupling, solved):
    red_blocks, link_total, size = inverse.shape[0], coupling.shape[1], inverse.shape[1]
    lanes = lax.broadcasted_iota(jnp.int32, (1, size), 1)
    values = []
    for i in range(red_blocks):
        mask = (lanes + i * size < live[0, level]).astype(jnp.float32)
        value = product(blocks[i] * mask, *halves(inverse[i]), 0) * mask
        solved[:, i * size : (i + 1) * size] = value
        values.append(value)
    ready()
    pushed = []
    for i in range(red_blocks):
        pairs = [halves(coupling[i, k]) for k in range(link_total)]
        high, low = (jnp.concatenate(part, 1) for part in zip(*pairs, strict=True))
        pushed.append(product(values[i], high, low, 0))
    for i in range(red_blocks):
        for k in range(link_total):
            target = red_blocks + links[i, k]
            blocks[target] = blocks[target] - pushed[i][:, k * size : (k + 1) * size]


def send_halves(place, level, blocks, red_blocks, kept, sent):
    half = kept.shape[0]
    upper = (place[0] >> level) & 1
    kept[...] = blocks[pl.ds(red_blocks + upper * half, half)]
    sent[...] = blocks[pl.ds(red_blocks + (1 - upper) * half, half)]


def load_halves(place, level, order, kept, received, joined, blocks):
    half = kept.shape[0]
    upper = (place[0] >> level) & 1
    joined[pl.ds(upper * half, half)] = kept[...]
    joined[pl.ds((1 - upper) * half, half)] = received[...]
    for n in range(2 * half):
        blocks[n] = joined[order[0, n]]


def lowest_kernel(place, live, links, section, inverse, coupling, solved, kept, sent, blocks):
    size = inverse.shape[1]
    for n in range(blocks.shape[0]):
        blocks[n] = section[:, n * size : (n + 1) * size]
    reduce_blocks(place[2], 0, live, links, blocks, inverse, coupling, solved)
    send_halves(place, 0, blocks, inverse.shape[0], kept, sent)


def middle_kernel(
    place, live, links, order, old, received, inverse, coupling, solved, kept, sent, joined, blocks
):
    load_halves(place, 0, order, old, received, joined, blocks)
    reduce_blocks(place[2], 1, live, links, blocks, inverse, coupling, solved)
    send_halves(place, 1, blocks, inverse.shape[0], kept, sent)


def highest_kernel(
    place, live, links, order, last_order, old, received, inverse, coupling, solved, kept, sent, joined, blocks
):
    load_halves(place, 1, order, old, received, joined, blocks)
    reduce_blocks(place[2], 2, live, links, blocks, inverse, coupling, solved)
    red_blocks, size = inverse.shape[0], inverse.shape[1]
    core = place[0] & 1
    for n in range(blocks.shape[0] - red_blocks):
        block = red_blocks + last_order[0, n]
        columns = slice(n * size, (n + 1) * size)
        for chip in range(kept.shape[0] // GROUP):
            rows = slice(chip * GROUP, (chip + 1) * GROUP)
            kept[rows, columns] = blocks[block, span(2 * chip + core, GROUP), :]
            sent[rows, columns] = blocks[block, span(2 * chip + 1 - core, GROUP), :]


def swap_chips(parts):
    return [parts[0]] + [flip(parts[f], "leaf", 2 * f) for f in range(1, len(parts))]


def solve_tree(right_sides, level_data, front_rows, root_inverse, root_coupling):
    leaf_count, col_count = lax.axis_size("leaf"), lax.axis_size("col")
    chip_count = leaf_count // 2
    panel_count, panel_rows, own_columns = root_inverse.shape
    group = GROUP * col_count
    rhs_rows = right_sides.shape[0]
    front_rows = front_rows.reshape(1, -1)
    red_blocks, size = level_data[0][0].shape[:2]
    solved = ((rhs_rows, red_blocks * size), jnp.float32)
    pair = ((2 * panel_rows, own_columns), jnp.bfloat16)
    one = ((group, own_columns), jnp.float32)
    more = ((group + GROUP, own_columns), jnp.float32)
    both = ((group, panel_count * panel_rows), jnp.float32)

    def halved(count):
        return (((count - red_blocks) // 2, rhs_rows, size), jnp.float32)

    def scratch(*shape):
        return pltpu.VMEM(shape, jnp.float32)

    inverse, coupling, links, order = level_data[0]
    count = right_sides.shape[1] // size
    solved_first, kept, sent, second = kernel_call(
        lowest_kernel,
        [solved, halved(count), halved(count)],
        [front_rows, links],
        [],
        loaded=[right_sides, inverse, coupling],
        late=1,
        stacks=[[(root_inverse, 1)]],
        scratch=[scratch(count, rhs_rows, size)],
        room=64,
    )
    received = flip(sent, "leaf", 1)
    far = flip(root_coupling, "leaf", 4)
    second_far = flip(second, "leaf", 4)
    near = flip(root_coupling, "leaf", 2)
    partner_inverse = flip(root_inverse, "leaf", 1)
    partner_coupling = flip(root_coupling, "leaf", 1)
    inverse, coupling, links, next_order = level_data[1]
    count -= red_blocks
    solved_second, kept, sent = kernel_call(
        middle_kernel,
        [solved, halved(count), halved(count)],
        [front_rows, links, order],
        [],
        loaded=[kept, received, inverse, coupling],
        late=1,
        held=[partner_inverse, partner_coupling],
        scratch=[scratch(count, rhs_rows, size)] * 2,
        room=64,
    )
    received = flip(sent, "leaf", 2)
    inverse, coupling, links, last_order = level_data[2]
    count -= red_blocks
    solved_third, kept, sent, near, second = kernel_call(
        highest_kernel,
        [solved, both, both],
        [front_rows, links, next_order, last_order],
        [],
        loaded=[kept, received, inverse, coupling],
        late=1,
        stacks=[[near], [(root_inverse, 1)]],
        held=[far],
        scratch=[scratch(count, rhs_rows, size)] * 2,
        room=64,
    )
    received = flip(sent, "leaf", 1)
    corner = flip(near, "leaf", 4)
    second_near = flip(second, "leaf", 2)
    partner_near = flip(near, "leaf", 1)
    (joined,) = kernel_call(join_kernel, [both], [], [kept, received], held=[partner_near, second_far])

    near_high, near_low = kernel_call(pair_kernel, [pair, pair], [], [], loaded=[(root_inverse, 0), (partner_inverse, 0)])
    parts = swap_columns([joined] * col_count)
    parts = kernel_call(
        first_kernel,
        [more] * chip_count,
        [],
        [*parts, near_high, near_low, kept, received],
        held=[corner, second_near],
        scratch=[scratch(col_count, group, own_columns)],
    )
    corner, far = gate([corner, far], [parts[-1]])
    partner_corner = flip(corner, "leaf", 1)
    partner_far = flip(far, "leaf", 1)
    parts = kernel_call(
        share_kernel,
        [more] * col_count,
        [],
        swap_chips(parts),
        held=[partner_far, partner_corner],
        scratch=[scratch(chip_count, GROUP, own_columns)],
    )
    (second_far,) = gate([second_far], [parts[-1]])
    second_corner = flip(second_far, "leaf", 2)
    partner_second = flip(second_far, "leaf", 1)
    between = assemble(
        [(root_coupling, None), (near, 0), (far, None), (corner, 0)]
        + [(partner_coupling, None), (partner_near, 0), (partner_far, None), (partner_corner, 0)]
    )
    first_sum = parts[0]
    parts = swap_columns(parts)
    (left,) = kernel_call(coupled_kernel, [one], [], [*parts, *between])
    second_near, second_corner = gate([second_near, second_corner], [left])
    panel = assemble(
        [(root_inverse, 1), (second_near, 0), (second_far, 0), (second_corner, 0)]
        + [(partner_inverse, 1), (flip(second_near, "leaf", 1), 0)]
        + [(partner_second, 0), (flip(second_corner, "leaf", 1), 0)]
    )
    parts = swap_columns([left] * col_count)
    parts = kernel_call(turn_kernel, [one] * col_count, [], [*parts, *panel])
    parts = swap_columns(parts)
    parts = kernel_call(back_kernel, [more] * col_count, [], [*parts, *between])
    parts = swap_columns(parts)
    parts = kernel_call(
        spread_kernel,
        [more] * chip_count,
        [],
        [*parts, first_sum],
        scratch=[scratch(col_count, GROUP, own_columns)],
    )
    *parts, last = kernel_call(
        last_kernel,
        [one] * (col_count + 1),
        [],
        [*swap_chips(parts), near_high, near_low],
        scratch=[scratch(col_count, group, own_columns)],
    )
    kept, sent = kernel_call(part_kernel, [both, both], [], [*swap_columns(parts), last])
    (result,) = kernel_call(
        merge_kernel,
        [((rhs_rows, panel_count, panel_rows), jnp.float32)],
        [],
        [kept, flip(sent, "leaf", 1)],
    )
    return (solved_first, solved_second, solved_third, result)


def replicates(rhs_rows, root_inverse):
    leaf_count, col_count = lax.axis_size("leaf"), lax.axis_size("col")
    panel_rows, own_columns = root_inverse.shape[1:]
    return (
        leaf_count == 8
        and col_count == 4
        and rhs_rows == GROUP * leaf_count
        and own_columns == 2 * panel_rows
    )


def local(
    right_sides,
    inverse_first,
    coupling_first,
    links_first,
    order_first,
    inverse_second,
    coupling_second,
    links_second,
    order_second,
    inverse_third,
    coupling_third,
    links_third,
    order_third,
    front_rows,
    root_inverse,
    root_coupling,
):
    level_data = (
        (inverse_first, coupling_first, links_first, order_first),
        (inverse_second, coupling_second, links_second, order_second),
        (inverse_third, coupling_third, links_third, order_third),
    )
    if replicates(right_sides.shape[0], root_inverse):
        return solve_tree(right_sides, level_data, front_rows, root_inverse, root_coupling)
    section = right_sides
    outputs = []
    for level_index in range(3):
        inverse, coupling, link_ids, order_map = level_data[level_index]
        solved, skeleton = eliminate(
            section, inverse, coupling, link_ids, front_rows[level_index, 0]
        )
        outputs.append(solved)
        if level_index < 2:
            skeleton = join_halves(skeleton, level_index)
        skeleton = jnp.take(skeleton, order_map[0], axis=1)
        section = skeleton.reshape(skeleton.shape[0], -1)
    return (*outputs, root_wide(section, root_inverse, root_coupling))


def solution(mesh):
    in_specs = (
        P("col", "leaf"),
        P("leaf", None, None),
        P("leaf", None, None, None),
        P("leaf", None),
        P("leaf", None),
        P("leaf", None, None),
        P("leaf", None, None, None),
        P("leaf", None),
        P("leaf", None),
        P("leaf", None, None),
        P("leaf", None, None, None),
        P("leaf", None),
        P("leaf", None),
        P(None, "leaf"),
        P(None, "leaf", "col"),
        P("leaf", "col"),
    )
    out_specs = (P("col", "leaf"), P("col", "leaf"), P("col", "leaf"), P("col", None, "leaf"))
    return jax.shard_map(local, mesh=mesh, in_specs=in_specs, out_specs=out_specs, check_vma=False)
```

```python
import jax
import jax.numpy as jnp
from jax import lax
from jax.experimental import pallas as pl
from jax.experimental.pallas import tpu as pltpu
from jax.sharding import PartitionSpec as P


def partner(block, axis, stride):
    count = lax.axis_size(axis)
    route = []
    for low in range(count):
        high = low | 1 << stride
        if high != low and high < count:
            route += [(low, high), (high, low)]
    return lax.ppermute(block, axis, route)


def eliminate(section, inverse, coupling, link_ids, live_count):
    block_rows = inverse.shape[-1]
    red_blocks = inverse.shape[0]
    link_total = coupling.shape[1]
    rhs_rows = section.shape[0]
    skeleton_count = section.shape[1] // block_rows - red_blocks
    redundant = section[:, : red_blocks * block_rows].reshape(rhs_rows, red_blocks, block_rows)
    positions = lax.broadcasted_iota(
        jnp.int32, (red_blocks, block_rows), 0
    ) * block_rows + lax.broadcasted_iota(jnp.int32, (red_blocks, block_rows), 1)
    live_rows = (positions < live_count).astype(jnp.float32)
    solved = (
        jnp.einsum("rib,iba->ria", redundant * live_rows, inverse, precision=lax.Precision.HIGHEST)
        * live_rows
    )
    pushed = jnp.einsum("ria,ikab->rikb", solved, coupling, precision=lax.Precision.HIGHEST)
    targets = (
        link_ids[:, :, None]
        == lax.broadcasted_iota(jnp.int32, (red_blocks, link_total, skeleton_count), 2)
    ).astype(jnp.float32)
    update = jnp.einsum("rikb,iks->rsb", pushed, targets, precision=lax.Precision.HIGHEST)
    skeleton = (
        section[:, red_blocks * block_rows :].reshape(rhs_rows, skeleton_count, block_rows) - update
    )
    return (solved.reshape(rhs_rows, red_blocks * block_rows), skeleton)


def join_halves(skeleton, level_index):
    half_blocks = skeleton.shape[1] // 2
    upper_half = lax.axis_index("leaf") >> level_index & 1
    kept_half = lax.dynamic_slice_in_dim(skeleton, upper_half * half_blocks, half_blocks, 1)
    sent_half = lax.dynamic_slice_in_dim(skeleton, (1 - upper_half) * half_blocks, half_blocks, 1)
    received = partner(sent_half, "leaf", level_index)
    return jnp.where(
        upper_half == 0,
        jnp.concatenate([kept_half, received], 1),
        jnp.concatenate([received, kept_half], 1),
    )


def spread_columns(values):
    return lax.all_gather(values, "col", axis=0, tiled=True)


def spread_leaf(values):
    return lax.all_gather(values, "leaf", axis=0, tiled=True)


def to_leaf_rows(values):
    full_rows = lax.all_gather(values, "col", axis=1, tiled=True)
    return lax.all_to_all(full_rows, "leaf", split_axis=1, concat_axis=0, tiled=True)


def to_column_rows(values):
    full_rows = lax.all_gather(values, "leaf", axis=1, tiled=True)
    return lax.all_to_all(full_rows, "col", split_axis=1, concat_axis=0, tiled=True)


def forward_product(values, matrix):
    return lax.psum_scatter(
        jnp.dot(
            values, matrix, precision=lax.Precision.HIGHEST, preferred_element_type=jnp.float32
        ),
        "leaf",
        scatter_dimension=0,
        tiled=True,
    )


def backward_product(values, matrix):
    return lax.psum_scatter(
        lax.dot_general(
            values,
            matrix,
            (((1,), (1,)), ((), ())),
            precision=lax.Precision.HIGHEST,
            preferred_element_type=jnp.float32,
        ),
        "col",
        scatter_dimension=0,
        tiled=True,
    )


def root_wide(section, root_inverse, root_coupling):
    rhs_rows = section.shape[0]
    panel_count = root_inverse.shape[0]
    panel_rows = root_inverse.shape[1]
    root_rhs = section.reshape(rhs_rows, panel_count, panel_rows)
    full_rhs = spread_columns(root_rhs)
    first_solve = forward_product(full_rhs[:, 0], root_inverse[0])
    coupled = forward_product(to_leaf_rows(first_solve), root_coupling)
    second_solve = forward_product(full_rhs[:, 1] - to_leaf_rows(coupled), root_inverse[1])
    forward_both = spread_leaf(jnp.stack([first_solve, second_solve], 1))
    last_panel = backward_product(forward_both[:, 1], root_inverse[1])
    back_coupled = backward_product(to_column_rows(last_panel), root_coupling)
    first_panel = backward_product(
        forward_both[:, 0] - to_column_rows(back_coupled), root_inverse[0]
    )
    root_solution = jnp.stack([first_panel, last_panel], 1)
    return root_solution


GROUP = 8


def flip(block, axis, distance):
    count = lax.axis_size(axis)
    return lax.ppermute(block, axis, [(i, i ^ distance) for i in range(count)])


def swap_columns(parts):
    return [parts[0]] + [flip(parts[e], "col", e) for e in range(1, len(parts))]


def kernel_call(
    body, out_shapes, scalars, operands, loaded=(), ahead=(), stacks=(), held=(), scratch=(), room=40, late=0
):
    vmem = pl.BlockSpec(memory_space=pltpu.VMEM)
    far = pl.BlockSpec(memory_space=pltpu.HBM)
    out_shapes = [jax.ShapeDtypeStruct(shape, kind) for shape, kind in out_shapes]
    plain = len(out_shapes)
    out_shapes += [jax.ShapeDtypeStruct(value.shape, value.dtype) for value in ahead]
    moves, pieces = [], []
    for n, stack in enumerate(stacks):
        first = 0
        for piece in stack:
            piece, index = piece if isinstance(piece, tuple) else (piece, None)
            size = piece.shape[0] if index is None and piece.ndim == 3 else None
            moves.append((n, first, size, index))
            pieces.append(piece)
            first += size or 1
        out_shapes.append(jax.ShapeDtypeStruct((first, *pieces[-1].shape[-2:]), pieces[-1].dtype))
    loaded = [value if isinstance(value, tuple) else (value, None) for value in loaded]
    early = len(scalars) + len(loaded)
    inputs = (len(scalars), len(loaded), len(ahead), len(pieces), len(held), len(operands))
    counts = (*inputs, plain, len(ahead), len(stacks), early)
    waits = early + len(ahead) + 2 * len(pieces)

    def run(*refs):
        groups, start = [], 0
        for count in (*counts, len(refs)):
            groups.append(refs[start : start + count])
            start += count
        ints, loads, nexts, sources, _, ins, outs, next_outs, targets, fetched, rest = groups
        if waits:
            *rest, sems = rest
        loads = [ref if i is None else ref.at[i] for ref, (_, i) in zip(loads, loaded, strict=True)]
        pairs = list(zip((*ints, *loads, *nexts), (*fetched, *next_outs), strict=True))
        staged = list(rest[len(rest) - len(moves) :])
        rest = rest[: len(rest) - len(moves)]
        for source, stage, (_, _, _, index) in zip(sources, staged, moves, strict=True):
            pairs.append((source if index is None else source.at[index], stage))
        ends = [
            (stage, targets[n].at[first if size is None else pl.ds(first, size)])
            for stage, (n, first, size, _) in zip(staged, moves, strict=True)
        ]
        copies = [
            pltpu.make_async_copy(*pair, sems.at[n]) for n, pair in enumerate((*pairs, *ends))
        ]
        leaving = copies[len(pairs) :]
        for copy in copies[: len(pairs)]:
            copy.start()
        for copy in copies[: early - late]:
            copy.wait()

        def ready():
            for copy in (*copies[early - late : early], *copies[len(pairs) - len(moves) : len(pairs)]):
                copy.wait()
            for copy in leaving:
                copy.start()

        place = (lax.axis_index("leaf"), lax.axis_index("col"), ready)
        if not late:
            ready()
        body(place, *fetched, *ins, *outs, *rest)
        for copy in (*copies[early : len(pairs) - len(moves)], *leaving):
            copy.wait()

    fetched = [pltpu.SMEM(value.shape, value.dtype) for value in scalars]
    fetched += [pltpu.VMEM(value.shape[i is not None :], value.dtype) for value, i in loaded]
    stages = [
        pltpu.VMEM(piece.shape[index is not None :], piece.dtype)
        for piece, (_, _, _, index) in zip(pieces, moves, strict=True)
    ]
    sems = [pltpu.SemaphoreType.DMA((waits,))] if waits else []
    return pl.pallas_call(
        run,
        out_shape=out_shapes,
        in_specs=[far] * sum(inputs[:-2])
        + [pl.BlockSpec(memory_space=pl.ANY)] * len(held)
        + [vmem] * len(operands),
        out_specs=[vmem] * (plain + len(ahead)) + [far] * len(stacks),
        scratch_shapes=fetched + list(scratch) + stages + sems,
        compiler_params=pltpu.CompilerParams(vmem_limit_bytes=room * 1024 * 1024),
    )(*scalars, *[value for value, _ in loaded], *ahead, *pieces, *held, *operands)


def halves(values):
    high = values.astype(jnp.bfloat16)
    return high, (values - high.astype(jnp.float32)).astype(jnp.bfloat16)


def product(values, high, low, contract):
    rows = values.shape[0]
    own_high, own_low = halves(values)
    dims = (((1,), (contract,)), ((), ()))
    both = lax.dot_general(
        jnp.concatenate([own_high, own_low], 0), high, dims, preferred_element_type=jnp.float32
    )
    cross = lax.dot_general(own_high, low, dims, preferred_element_type=jnp.float32)
    return both[:rows] + both[rows:] + cross


def regroup(values, distance, parts):
    if distance == 0:
        return values
    size = values.shape[0] // parts
    return jnp.concatenate(
        [values[(d ^ distance) * size : (d ^ distance) * size + size] for d in range(parts)], 0
    )


def span(index, size):
    return pl.ds(pl.multiple_of(index * size, size), size)


def gate(values, after):
    far = pl.BlockSpec(memory_space=pltpu.HBM)

    def run(*refs):
        pass

    return pl.pallas_call(
        run,
        out_shape=[jax.ShapeDtypeStruct(value.shape, value.dtype) for value in values],
        in_specs=[far] * len(values) + [pl.BlockSpec(memory_space=pltpu.VMEM)] * len(after),
        out_specs=[far] * len(values),
        input_output_aliases={n: n for n in range(len(values))},
        compiler_params=pltpu.CompilerParams(vmem_limit_bytes=1024 * 1024),
    )(*values, *after)


def join_kernel(place, kept, received, joined):
    half = kept.shape[1] // 2
    joined[:, :half] = kept[:, :half]
    joined[:, half:] = received[:, :half]


def assemble_kernel(place, *refs):
    *blocks, high, low = refs
    rows = blocks[0].shape[0]
    for n, block in enumerate(blocks):
        core, chip = divmod(n, len(blocks) // 2)
        where = span(place[0] ^ core ^ 2 * chip, rows)
        high[where, :], low[where, :] = halves(block[...])


def assemble(parts, stacks=()):
    rows, width = parts[0][0].shape[-2:]
    panel = ((rows * lax.axis_size("leaf"), width), jnp.bfloat16)
    return kernel_call(assemble_kernel, [panel, panel], [], [], loaded=parts, stacks=stacks)


def pair_kernel(place, *refs):
    *blocks, high, low = refs
    rows, width = blocks[0].shape
    for n, block in enumerate(blocks):
        where = slice(n % 2 * rows, (n % 2 + 1) * rows), slice(n // 2 * width, (n // 2 + 1) * width)
        high[where], low[where] = halves(block[...])


def first_kernel(place, *refs):
    count = (len(refs) - 5) // 2
    parts, (high, low, kept, received) = refs[:count], refs[count : count + 4]
    sent, pushed = refs[count + 4 : -1], refs[-1]
    rows, width = parts[0].shape
    values = product(jnp.concatenate([part[...] for part in parts], 0), high[...], low[...], 0)
    for e in range(count):
        pushed[e] = values[e * rows : (e + 1) * rows]
    chip, lower = place[0] >> 1, (place[0] & 1) == 0
    half = width // 2
    for f, part in enumerate(sent):
        where = span(chip ^ f, GROUP)
        for e in range(count):
            part[e * GROUP : (e + 1) * GROUP, :] = pushed[e, where, :]
        own, other = kept[where, half:], received[where, half:]
        part[rows:, :half] = jnp.where(lower, own, other)
        part[rows:, half:] = jnp.where(lower, other, own)


def share_kernel(place, *refs):
    count = (len(refs) - 1) // 2
    parts, sent, rest = refs[:count], refs[count:-1], refs[-1]
    rows = parts[0].shape[0] - GROUP
    total = sum(part[:rows, :] for part in parts[1:]) + parts[0][:rows, :]
    for f, part in enumerate(parts):
        rest[f] = part[rows:, :]
    for e, part in enumerate(sent):
        part[:rows, :] = total
        part[rows:, :] = rest[(place[0] >> 1) ^ place[1] ^ e]


def gathered_product(place, parts, high, low):
    count = len(parts)
    width = parts[0].shape[1]
    total = None
    for e, part in enumerate(parts):
        rows = span(place[1] ^ e, width)
        values = part[: count * GROUP, :]
        term = product(regroup(values, e, count), high[rows, :], low[rows, :], 0)
        total = term if total is None else total + term
    return total


def coupled_kernel(place, *refs):
    parts, (high, low, result, first) = refs[:-4], refs[-4:]
    rest = jnp.concatenate([part[len(parts) * GROUP :, :] for part in parts], 0)
    result[...] = rest - gathered_product(place, parts, high, low)
    for n in range(4):
        start = (n // 2 ^ n % 2 * 2) * GROUP
        first[n * GROUP : (n + 1) * GROUP, :] = parts[n // 2][start : start + GROUP, :]


def scatter_product(place, values, high, low, sent):
    count = len(sent)
    width = sent[0].shape[1]
    for e, part in enumerate(sent):
        rows = span(place[1] ^ e, width)
        part[...] = regroup(product(values, high[rows, :], low[rows, :], 1), e, count)


def turn_kernel(place, *refs):
    count = (len(refs) - 2) // 2
    parts, (high, low), sent = refs[:count], refs[count : count + 2], refs[count + 2 :]
    second = gathered_product(place, parts, high, low)
    scatter_product(place, second, high, low, sent)


def back_kernel(place, *refs):
    count = (len(refs) - 2) // 2
    parts, (high, low), sent = refs[:count], refs[count : count + 2], refs[count + 2 :]
    total = sum(part[...] for part in parts[1:]) + parts[0][...]
    rows, width = total.shape
    values = []
    for g in range(count):
        where = span(place[1] ^ g, width)
        values.append(product(total, high[where, :], low[where, :], 1))
    for e, part in enumerate(sent):
        for n in range(count):
            start = (e ^ n % 2 * 2) * GROUP
            part[n * GROUP : (n + 1) * GROUP, :] = values[e ^ n // 2][start : start + GROUP]
        part[rows:, :] = total[e * GROUP : (e + 1) * GROUP]


def spread_kernel(place, *refs):
    count = (len(refs) - 2) // 2
    parts, first, sent, rest = refs[:count], refs[count], refs[count + 1 : -1], refs[-1]
    rows = parts[0].shape[0] - GROUP
    total = sum(part[:rows, :] for part in parts[1:]) + parts[0][:rows, :]
    for e, part in enumerate(parts):
        rest[e] = part[rows:, :]
    for f, part in enumerate(sent):
        part[:rows, :] = first[:rows, :] - total
        part[rows:, :] = rest[(place[0] >> 1) ^ place[1] ^ f]


def last_kernel(place, *refs):
    *parts, high, low, own, other, last, joined = refs
    rows = own.shape[0]
    chip = place[0] >> 1
    for f, part in enumerate(parts):
        where = span(chip ^ f, GROUP)
        for n in range(4):
            joined[n, where, :] = part[n * GROUP : (n + 1) * GROUP, :]
        last[where, :] = part[rows:, :]
    columns = [jnp.concatenate([joined[n], joined[n + 1]], 0) for n in (0, 2)]
    values = product(jnp.concatenate(columns, 1), high[...], low[...], 1)
    own[...] = values[:rows]
    other[...] = values[rows:]


def part_kernel(place, *refs):
    own, other, last, kept, sent = refs
    total = own[...] + other[...]
    half = total.shape[1] // 2
    lower = (place[0] & 1) == 0
    for n, panel in enumerate((total, last[...])):
        own, other = panel[:, :half], panel[:, half:]
        if n:
            own, other = jnp.where(lower, own, other), jnp.where(lower, other, own)
        kept[:, n * half : (n + 1) * half] = own
        sent[:, n * half : (n + 1) * half] = other


def merge_kernel(place, kept, received, result):
    panels, half = result.shape[1:]
    lower = (place[0] & 1) == 0
    for chip in range(kept.shape[0] // GROUP):
        rows = slice(chip * GROUP, (chip + 1) * GROUP)
        for n in range(panels):
            columns = slice(n * half, (n + 1) * half)
            own, other = kept[rows, columns], received[rows, columns]
            start = 2 * chip * GROUP
            result[start : start + GROUP, n, :] = jnp.where(lower, own, other)
            result[start + GROUP : start + 2 * GROUP, n, :] = jnp.where(lower, other, own)


def reduce_blocks(ready, level, live, links, blocks, inverse, coupling, solved):
    red_blocks, link_total, size = inverse.shape[0], coupling.shape[1], inverse.shape[1]
    lanes = lax.broadcasted_iota(jnp.int32, (1, size), 1)
    values = []
    for i in range(red_blocks):
        mask = (lanes + i * size < live[0, level]).astype(jnp.float32)
        value = product(blocks[i] * mask, *halves(inverse[i]), 0) * mask
        solved[:, i * size : (i + 1) * size] = value
        values.append(value)
    ready()
    pushed = []
    for i in range(red_blocks):
        pairs = [halves(coupling[i, k]) for k in range(link_total)]
        high, low = (jnp.concatenate(part, 1) for part in zip(*pairs, strict=True))
        pushed.append(product(values[i], high, low, 0))
    for i in range(red_blocks):
        for k in range(link_total):
            target = red_blocks + links[i, k]
            blocks[target] = blocks[target] - pushed[i][:, k * size : (k + 1) * size]


def send_halves(place, level, blocks, red_blocks, kept, sent):
    half = kept.shape[0]
    upper = (place[0] >> level) & 1
    kept[...] = blocks[pl.ds(red_blocks + upper * half, half)]
    sent[...] = blocks[pl.ds(red_blocks + (1 - upper) * half, half)]


def load_halves(place, level, order, kept, received, joined, blocks):
    half = kept.shape[0]
    upper = (place[0] >> level) & 1
    joined[pl.ds(upper * half, half)] = kept[...]
    joined[pl.ds((1 - upper) * half, half)] = received[...]
    for n in range(2 * half):
        blocks[n] = joined[order[0, n]]


def lowest_kernel(place, live, links, section, inverse, coupling, solved, kept, sent, blocks):
    size = inverse.shape[1]
    for n in range(blocks.shape[0]):
        blocks[n] = section[:, n * size : (n + 1) * size]
    reduce_blocks(place[2], 0, live, links, blocks, inverse, coupling, solved)
    send_halves(place, 0, blocks, inverse.shape[0], kept, sent)


def middle_kernel(
    place, live, links, order, old, received, inverse, coupling, solved, kept, sent, joined, blocks
):
    load_halves(place, 0, order, old, received, joined, blocks)
    reduce_blocks(place[2], 1, live, links, blocks, inverse, coupling, solved)
    send_halves(place, 1, blocks, inverse.shape[0], kept, sent)


def highest_kernel(
    place, live, links, order, last_order, old, received, inverse, coupling, solved, kept, sent, joined, blocks
):
    load_halves(place, 1, order, old, received, joined, blocks)
    reduce_blocks(place[2], 2, live, links, blocks, inverse, coupling, solved)
    red_blocks, size = inverse.shape[0], inverse.shape[1]
    core = place[0] & 1
    for n in range(blocks.shape[0] - red_blocks):
        block = red_blocks + last_order[0, n]
        columns = slice(n * size, (n + 1) * size)
        for chip in range(kept.shape[0] // GROUP):
            rows = slice(chip * GROUP, (chip + 1) * GROUP)
            kept[rows, columns] = blocks[block, span(2 * chip + core, GROUP), :]
            sent[rows, columns] = blocks[block, span(2 * chip + 1 - core, GROUP), :]


def swap_chips(parts):
    return [parts[0]] + [flip(parts[f], "leaf", 2 * f) for f in range(1, len(parts))]


def solve_tree(right_sides, level_data, front_rows, root_inverse, root_coupling):
    leaf_count, col_count = lax.axis_size("leaf"), lax.axis_size("col")
    chip_count = leaf_count // 2
    panel_count, panel_rows, own_columns = root_inverse.shape
    group = GROUP * col_count
    rhs_rows = right_sides.shape[0]
    front_rows = front_rows.reshape(1, -1)
    red_blocks, size = level_data[0][0].shape[:2]
    solved = ((rhs_rows, red_blocks * size), jnp.float32)
    pair = ((2 * panel_rows, own_columns), jnp.bfloat16)
    wide = ((2 * panel_rows, 2 * own_columns), jnp.bfloat16)
    one = ((group, own_columns), jnp.float32)
    more = ((group + GROUP, own_columns), jnp.float32)
    both = ((group, panel_count * panel_rows), jnp.float32)

    def halved(count):
        return (((count - red_blocks) // 2, rhs_rows, size), jnp.float32)

    def scratch(*shape):
        return pltpu.VMEM(shape, jnp.float32)

    inverse, coupling, links, order = level_data[0]
    count = right_sides.shape[1] // size
    solved_first, kept, sent, second, first = kernel_call(
        lowest_kernel,
        [solved, halved(count), halved(count)],
        [front_rows, links],
        [],
        loaded=[right_sides, inverse, coupling],
        late=1,
        stacks=[[(root_inverse, 1)], [(root_inverse, 0)]],
        scratch=[scratch(count, rhs_rows, size)],
        room=64,
    )
    received = flip(sent, "leaf", 1)
    far = flip(root_coupling, "leaf", 4)
    second_far = flip(second, "leaf", 4)
    near = flip(root_coupling, "leaf", 2)
    first = flip(first, "col", 1)
    partner_inverse = flip(root_inverse, "leaf", 1)
    partner_coupling = flip(root_coupling, "leaf", 1)
    inverse, coupling, links, next_order = level_data[1]
    count -= red_blocks
    solved_second, kept, sent = kernel_call(
        middle_kernel,
        [solved, halved(count), halved(count)],
        [front_rows, links, order],
        [],
        loaded=[kept, received, inverse, coupling],
        late=1,
        held=[partner_inverse, partner_coupling],
        scratch=[scratch(count, rhs_rows, size)] * 2,
        room=64,
    )
    received = flip(sent, "leaf", 2)
    inverse, coupling, links, last_order = level_data[2]
    count -= red_blocks
    solved_third, kept, sent, near, second = kernel_call(
        highest_kernel,
        [solved, both, both],
        [front_rows, links, next_order, last_order],
        [],
        loaded=[kept, received, inverse, coupling],
        late=1,
        stacks=[[near], [(root_inverse, 1)]],
        held=[far],
        scratch=[scratch(count, rhs_rows, size)] * 2,
        room=64,
    )
    received = flip(sent, "leaf", 1)
    corner = flip(near, "leaf", 4)
    second_near = flip(second, "leaf", 2)
    (joined,) = kernel_call(join_kernel, [both], [], [kept, received], held=[second_far, first])

    near_high, near_low = kernel_call(pair_kernel, [pair, pair], [], [], loaded=[(root_inverse, 0), (partner_inverse, 0)])
    parts = swap_columns([joined] * col_count)
    parts = kernel_call(
        first_kernel,
        [more] * chip_count,
        [],
        [*parts, near_high, near_low, kept, received],
        held=[corner, second_near],
        scratch=[scratch(col_count, group, own_columns)],
    )
    corner, far = gate([corner, far], [parts[-1]])
    partner_corner = flip(corner, "leaf", 1)
    partner_far = flip(far, "leaf", 1)
    parts = swap_chips(parts)
    parts = kernel_call(
        share_kernel,
        [more] * col_count,
        [],
        parts,
        held=[partner_corner],
        scratch=[scratch(chip_count, GROUP, own_columns)],
    )
    second_near, near = gate([second_near, near], [parts[-1]])
    second_corner = flip(second_near, "leaf", 4)
    partner_near = flip(near, "leaf", 1)
    *between, sides = assemble(
        [(root_coupling, None), (near, 0), (far, None), (corner, 0)]
        + [(partner_coupling, None), (partner_near, 0), (partner_far, None), (partner_corner, 0)],
        stacks=[[second_near, second_far]],
    )
    parts = swap_columns(parts)
    left, first_sum = kernel_call(coupled_kernel, [one, one], [], [*parts, *between])
    sides, second_corner = gate([sides, second_corner], [left])
    partner_sides = flip(sides, "leaf", 1)
    panel = assemble(
        [(root_inverse, 1), (sides, 0), (sides, 1), (second_corner, 0)]
        + [(partner_inverse, 1), (partner_sides, 0), (partner_sides, 1)]
        + [(flip(second_corner, "leaf", 1), 0)]
    )
    parts = swap_columns([left] * col_count)
    parts = kernel_call(turn_kernel, [one] * col_count, [], [*parts, *panel])
    parts = swap_columns(parts)
    parts = kernel_call(back_kernel, [more] * col_count, [], [*parts, *between])
    parts = swap_columns(parts)
    parts = kernel_call(
        spread_kernel,
        [more] * chip_count,
        [],
        [*parts, first_sum],
        scratch=[scratch(col_count, GROUP, own_columns)],
    )
    (first,) = gate([first], [parts[-1]])
    first_high, first_low = kernel_call(
        pair_kernel,
        [wide, wide],
        [],
        [],
        loaded=[(root_inverse, 0), (partner_inverse, 0), (first, 0), (flip(first, "leaf", 1), 0)],
    )
    own, other, last = kernel_call(
        last_kernel,
        [one, one, one],
        [],
        [*swap_chips(parts), first_high, first_low],
        scratch=[scratch(col_count, group, own_columns)],
    )
    kept, sent = kernel_call(part_kernel, [both, both], [], [own, flip(other, "col", 2), last])
    (result,) = kernel_call(
        merge_kernel,
        [((rhs_rows, panel_count, panel_rows), jnp.float32)],
        [],
        [kept, flip(sent, "leaf", 1)],
    )
    return (solved_first, solved_second, solved_third, result)


def replicates(rhs_rows, root_inverse):
    leaf_count, col_count = lax.axis_size("leaf"), lax.axis_size("col")
    panel_rows, own_columns = root_inverse.shape[1:]
    return (
        leaf_count == 8
        and col_count == 4
        and rhs_rows == GROUP * leaf_count
        and own_columns == 2 * panel_rows
    )


def local(
    right_sides,
    inverse_first,
    coupling_first,
    links_first,
    order_first,
    inverse_second,
    coupling_second,
    links_second,
    order_second,
    inverse_third,
    coupling_third,
    links_third,
    order_third,
    front_rows,
    root_inverse,
    root_coupling,
):
    level_data = (
        (inverse_first, coupling_first, links_first, order_first),
        (inverse_second, coupling_second, links_second, order_second),
        (inverse_third, coupling_third, links_third, order_third),
    )
    if replicates(right_sides.shape[0], root_inverse):
        return solve_tree(right_sides, level_data, front_rows, root_inverse, root_coupling)
    section = right_sides
    outputs = []
    for level_index in range(3):
        inverse, coupling, link_ids, order_map = level_data[level_index]
        solved, skeleton = eliminate(
            section, inverse, coupling, link_ids, front_rows[level_index, 0]
        )
        outputs.append(solved)
        if level_index < 2:
            skeleton = join_halves(skeleton, level_index)
        skeleton = jnp.take(skeleton, order_map[0], axis=1)
        section = skeleton.reshape(skeleton.shape[0], -1)
    return (*outputs, root_wide(section, root_inverse, root_coupling))


def solution(mesh):
    in_specs = (
        P("col", "leaf"),
        P("leaf", None, None),
        P("leaf", None, None, None),
        P("leaf", None),
        P("leaf", None),
        P("leaf", None, None),
        P("leaf", None, None, None),
        P("leaf", None),
        P("leaf", None),
        P("leaf", None, None),
        P("leaf", None, None, None),
        P("leaf", None),
        P("leaf", None),
        P(None, "leaf"),
        P(None, "leaf", "col"),
        P("leaf", "col"),
    )
    out_specs = (P("col", "leaf"), P("col", "leaf"), P("col", "leaf"), P("col", None, "leaf"))
    return jax.shard_map(local, mesh=mesh, in_specs=in_specs, out_specs=out_specs, check_vma=False)
```

```python
import jax
import jax.numpy as jnp
from jax import lax
from jax.experimental import pallas as pl
from jax.experimental.pallas import tpu as pltpu
from jax.sharding import PartitionSpec as P


def partner(block, axis, stride):
    count = lax.axis_size(axis)
    route = []
    for low in range(count):
        high = low | 1 << stride
        if high != low and high < count:
            route += [(low, high), (high, low)]
    return lax.ppermute(block, axis, route)


def eliminate(section, inverse, coupling, link_ids, live_count):
    block_rows = inverse.shape[-1]
    red_blocks = inverse.shape[0]
    link_total = coupling.shape[1]
    rhs_rows = section.shape[0]
    skeleton_count = section.shape[1] // block_rows - red_blocks
    redundant = section[:, : red_blocks * block_rows].reshape(rhs_rows, red_blocks, block_rows)
    positions = lax.broadcasted_iota(
        jnp.int32, (red_blocks, block_rows), 0
    ) * block_rows + lax.broadcasted_iota(jnp.int32, (red_blocks, block_rows), 1)
    live_rows = (positions < live_count).astype(jnp.float32)
    solved = (
        jnp.einsum("rib,iba->ria", redundant * live_rows, inverse, precision=lax.Precision.HIGHEST)
        * live_rows
    )
    pushed = jnp.einsum("ria,ikab->rikb", solved, coupling, precision=lax.Precision.HIGHEST)
    targets = (
        link_ids[:, :, None]
        == lax.broadcasted_iota(jnp.int32, (red_blocks, link_total, skeleton_count), 2)
    ).astype(jnp.float32)
    update = jnp.einsum("rikb,iks->rsb", pushed, targets, precision=lax.Precision.HIGHEST)
    skeleton = (
        section[:, red_blocks * block_rows :].reshape(rhs_rows, skeleton_count, block_rows) - update
    )
    return (solved.reshape(rhs_rows, red_blocks * block_rows), skeleton)


def join_halves(skeleton, level_index):
    half_blocks = skeleton.shape[1] // 2
    upper_half = lax.axis_index("leaf") >> level_index & 1
    kept_half = lax.dynamic_slice_in_dim(skeleton, upper_half * half_blocks, half_blocks, 1)
    sent_half = lax.dynamic_slice_in_dim(skeleton, (1 - upper_half) * half_blocks, half_blocks, 1)
    received = partner(sent_half, "leaf", level_index)
    return jnp.where(
        upper_half == 0,
        jnp.concatenate([kept_half, received], 1),
        jnp.concatenate([received, kept_half], 1),
    )


def spread_columns(values):
    return lax.all_gather(values, "col", axis=0, tiled=True)


def spread_leaf(values):
    return lax.all_gather(values, "leaf", axis=0, tiled=True)


def to_leaf_rows(values):
    full_rows = lax.all_gather(values, "col", axis=1, tiled=True)
    return lax.all_to_all(full_rows, "leaf", split_axis=1, concat_axis=0, tiled=True)


def to_column_rows(values):
    full_rows = lax.all_gather(values, "leaf", axis=1, tiled=True)
    return lax.all_to_all(full_rows, "col", split_axis=1, concat_axis=0, tiled=True)


def forward_product(values, matrix):
    return lax.psum_scatter(
        jnp.dot(
            values, matrix, precision=lax.Precision.HIGHEST, preferred_element_type=jnp.float32
        ),
        "leaf",
        scatter_dimension=0,
        tiled=True,
    )


def backward_product(values, matrix):
    return lax.psum_scatter(
        lax.dot_general(
            values,
            matrix,
            (((1,), (1,)), ((), ())),
            precision=lax.Precision.HIGHEST,
            preferred_element_type=jnp.float32,
        ),
        "col",
        scatter_dimension=0,
        tiled=True,
    )


def root_wide(section, root_inverse, root_coupling):
    rhs_rows = section.shape[0]
    panel_count = root_inverse.shape[0]
    panel_rows = root_inverse.shape[1]
    root_rhs = section.reshape(rhs_rows, panel_count, panel_rows)
    full_rhs = spread_columns(root_rhs)
    first_solve = forward_product(full_rhs[:, 0], root_inverse[0])
    coupled = forward_product(to_leaf_rows(first_solve), root_coupling)
    second_solve = forward_product(full_rhs[:, 1] - to_leaf_rows(coupled), root_inverse[1])
    forward_both = spread_leaf(jnp.stack([first_solve, second_solve], 1))
    last_panel = backward_product(forward_both[:, 1], root_inverse[1])
    back_coupled = backward_product(to_column_rows(last_panel), root_coupling)
    first_panel = backward_product(
        forward_both[:, 0] - to_column_rows(back_coupled), root_inverse[0]
    )
    root_solution = jnp.stack([first_panel, last_panel], 1)
    return root_solution


GROUP = 8


def flip(block, axis, distance):
    count = lax.axis_size(axis)
    return lax.ppermute(block, axis, [(i, i ^ distance) for i in range(count)])


def swap_columns(parts):
    return [parts[0]] + [flip(parts[e], "col", e) for e in range(1, len(parts))]


def kernel_call(
    body, out_shapes, scalars, operands, loaded=(), ahead=(), stacks=(), held=(), scratch=(), room=40, late=0
):
    vmem = pl.BlockSpec(memory_space=pltpu.VMEM)
    far = pl.BlockSpec(memory_space=pltpu.HBM)
    out_shapes = [jax.ShapeDtypeStruct(shape, kind) for shape, kind in out_shapes]
    plain = len(out_shapes)
    out_shapes += [jax.ShapeDtypeStruct(value.shape, value.dtype) for value in ahead]
    moves, pieces = [], []
    for n, stack in enumerate(stacks):
        first = 0
        for piece in stack:
            piece, index = piece if isinstance(piece, tuple) else (piece, None)
            size = piece.shape[0] if index is None and piece.ndim == 3 else None
            moves.append((n, first, size, index))
            pieces.append(piece)
            first += size or 1
        out_shapes.append(jax.ShapeDtypeStruct((first, *pieces[-1].shape[-2:]), pieces[-1].dtype))
    loaded = [value if isinstance(value, tuple) else (value, None) for value in loaded]
    early = len(scalars) + len(loaded)
    inputs = (len(scalars), len(loaded), len(ahead), len(pieces), len(held), len(operands))
    counts = (*inputs, plain, len(ahead), len(stacks), early)
    waits = early + len(ahead) + 2 * len(pieces)

    def run(*refs):
        groups, start = [], 0
        for count in (*counts, len(refs)):
            groups.append(refs[start : start + count])
            start += count
        ints, loads, nexts, sources, _, ins, outs, next_outs, targets, fetched, rest = groups
        if waits:
            *rest, sems = rest
        loads = [ref if i is None else ref.at[i] for ref, (_, i) in zip(loads, loaded, strict=True)]
        pairs = list(zip((*ints, *loads, *nexts), (*fetched, *next_outs), strict=True))
        staged = list(rest[len(rest) - len(moves) :])
        rest = rest[: len(rest) - len(moves)]
        for source, stage, (_, _, _, index) in zip(sources, staged, moves, strict=True):
            pairs.append((source if index is None else source.at[index], stage))
        ends = [
            (stage, targets[n].at[first if size is None else pl.ds(first, size)])
            for stage, (n, first, size, _) in zip(staged, moves, strict=True)
        ]
        copies = [
            pltpu.make_async_copy(*pair, sems.at[n]) for n, pair in enumerate((*pairs, *ends))
        ]
        leaving = copies[len(pairs) :]
        for copy in copies[: len(pairs)]:
            copy.start()
        for copy in copies[: early - late]:
            copy.wait()

        def ready():
            for copy in (*copies[early - late : early], *copies[len(pairs) - len(moves) : len(pairs)]):
                copy.wait()
            for copy in leaving:
                copy.start()

        place = (lax.axis_index("leaf"), lax.axis_index("col"), ready)
        if not late:
            ready()
        body(place, *fetched, *ins, *outs, *rest)
        for copy in (*copies[early : len(pairs) - len(moves)], *leaving):
            copy.wait()

    fetched = [pltpu.SMEM(value.shape, value.dtype) for value in scalars]
    fetched += [pltpu.VMEM(value.shape[i is not None :], value.dtype) for value, i in loaded]
    stages = [
        pltpu.VMEM(piece.shape[index is not None :], piece.dtype)
        for piece, (_, _, _, index) in zip(pieces, moves, strict=True)
    ]
    sems = [pltpu.SemaphoreType.DMA((waits,))] if waits else []
    return pl.pallas_call(
        run,
        out_shape=out_shapes,
        in_specs=[far] * sum(inputs[:-2])
        + [pl.BlockSpec(memory_space=pl.ANY)] * len(held)
        + [vmem] * len(operands),
        out_specs=[vmem] * (plain + len(ahead)) + [far] * len(stacks),
        scratch_shapes=fetched + list(scratch) + stages + sems,
        compiler_params=pltpu.CompilerParams(vmem_limit_bytes=room * 1024 * 1024),
    )(*scalars, *[value for value, _ in loaded], *ahead, *pieces, *held, *operands)


def halves(values):
    high = values.astype(jnp.bfloat16)
    return high, (values - high.astype(jnp.float32)).astype(jnp.bfloat16)


def product(values, high, low, contract):
    rows = values.shape[0]
    own_high, own_low = halves(values)
    dims = (((1,), (contract,)), ((), ()))
    both = lax.dot_general(
        jnp.concatenate([own_high, own_low], 0), high, dims, preferred_element_type=jnp.float32
    )
    cross = lax.dot_general(own_high, low, dims, preferred_element_type=jnp.float32)
    return both[:rows] + both[rows:] + cross


def regroup(values, distance, parts):
    if distance == 0:
        return values
    size = values.shape[0] // parts
    return jnp.concatenate(
        [values[(d ^ distance) * size : (d ^ distance) * size + size] for d in range(parts)], 0
    )


def span(index, size):
    return pl.ds(pl.multiple_of(index * size, size), size)


def gate(values, after):
    far = pl.BlockSpec(memory_space=pltpu.HBM)

    def run(*refs):
        pass

    return pl.pallas_call(
        run,
        out_shape=[jax.ShapeDtypeStruct(value.shape, value.dtype) for value in values],
        in_specs=[far] * len(values) + [pl.BlockSpec(memory_space=pltpu.VMEM)] * len(after),
        out_specs=[far] * len(values),
        input_output_aliases={n: n for n in range(len(values))},
        compiler_params=pltpu.CompilerParams(vmem_limit_bytes=1024 * 1024),
    )(*values, *after)


def join_kernel(place, kept, received, joined):
    half = kept.shape[1] // 2
    joined[:, :half] = kept[:, :half]
    joined[:, half:] = received[:, :half]


def assemble_kernel(place, *refs):
    *blocks, high, low = refs
    rows = blocks[0].shape[0]
    for n, block in enumerate(blocks):
        core, chip = divmod(n, len(blocks) // 2)
        where = span(place[0] ^ core ^ 2 * chip, rows)
        high[where, :], low[where, :] = halves(block[...])


def assemble(parts, stacks=()):
    rows, width = parts[0][0].shape[-2:]
    panel = ((rows * lax.axis_size("leaf"), width), jnp.bfloat16)
    return kernel_call(assemble_kernel, [panel, panel], [], [], loaded=parts, stacks=stacks)


def pair_kernel(place, *refs):
    *blocks, high, low = refs
    rows, width = blocks[0].shape
    for n, block in enumerate(blocks):
        where = slice(n % 2 * rows, (n % 2 + 1) * rows), slice(n // 2 * width, (n // 2 + 1) * width)
        high[where], low[where] = halves(block[...])


def first_kernel(place, *refs):
    count = (len(refs) - 5) // 2
    parts, (high, low, kept, received) = refs[:count], refs[count : count + 4]
    sent, pushed = refs[count + 4 : -1], refs[-1]
    rows, width = parts[0].shape
    values = product(jnp.concatenate([part[...] for part in parts], 0), high[...], low[...], 0)
    for e in range(count):
        pushed[e] = values[e * rows : (e + 1) * rows]
    chip, lower = place[0] >> 1, (place[0] & 1) == 0
    half = width // 2
    for f, part in enumerate(sent):
        where = span(chip ^ f, GROUP)
        for e in range(count):
            part[e * GROUP : (e + 1) * GROUP, :] = pushed[e, where, :]
        own, other = kept[where, half:], received[where, half:]
        part[rows:, :half] = jnp.where(lower, own, other)
        part[rows:, half:] = jnp.where(lower, other, own)


def share_kernel(place, *refs):
    count = (len(refs) - 1) // 2
    parts, sent, rest = refs[:count], refs[count:-1], refs[-1]
    rows = parts[0].shape[0] - GROUP
    total = sum(part[:rows, :] for part in parts[1:]) + parts[0][:rows, :]
    for f, part in enumerate(parts):
        rest[f] = part[rows:, :]
    for e, part in enumerate(sent):
        part[:rows, :] = total
        part[rows:, :] = rest[(place[0] >> 1) ^ place[1] ^ e]


def gathered_product(place, parts, high, low):
    count = len(parts)
    width = parts[0].shape[1]
    total = None
    for e, part in enumerate(parts):
        rows = span(place[1] ^ e, width)
        values = part[: count * GROUP, :]
        term = product(regroup(values, e, count), high[rows, :], low[rows, :], 0)
        total = term if total is None else total + term
    return total


def coupled_kernel(place, *refs):
    parts, (high, low, result, first) = refs[:-4], refs[-4:]
    rest = jnp.concatenate([part[len(parts) * GROUP :, :] for part in parts], 0)
    result[...] = rest - gathered_product(place, parts, high, low)
    for n in range(4):
        start = (n // 2 ^ n % 2 * 2) * GROUP
        first[n * GROUP : (n + 1) * GROUP, :] = parts[n // 2][start : start + GROUP, :]


def scatter_product(place, values, high, low, sent):
    count = len(sent)
    width = sent[0].shape[1]
    for e, part in enumerate(sent):
        rows = span(place[1] ^ e, width)
        part[...] = regroup(product(values, high[rows, :], low[rows, :], 1), e, count)


def turn_kernel(place, *refs):
    count = (len(refs) - 2) // 2
    parts, (high, low), sent = refs[:count], refs[count : count + 2], refs[count + 2 :]
    second = gathered_product(place, parts, high, low)
    scatter_product(place, second, high, low, sent)


def back_kernel(place, *refs):
    count = (len(refs) - 2) // 2
    parts, (high, low), sent = refs[:count], refs[count : count + 2], refs[count + 2 :]
    total = sum(part[...] for part in parts[1:]) + parts[0][...]
    rows, width = total.shape
    values = []
    for g in range(count):
        where = span(place[1] ^ g, width)
        values.append(product(total, high[where, :], low[where, :], 1))
    for e, part in enumerate(sent):
        for n in range(count):
            start = (e ^ n % 2 * 2) * GROUP
            part[n * GROUP : (n + 1) * GROUP, :] = values[e ^ n // 2][start : start + GROUP]
        part[rows:, :] = total[e * GROUP : (e + 1) * GROUP]


def spread_kernel(place, *refs):
    count = (len(refs) - 2) // 2
    parts, first, sent, rest = refs[:count], refs[count], refs[count + 1 : -1], refs[-1]
    rows = parts[0].shape[0] - GROUP
    total = sum(part[:rows, :] for part in parts[1:]) + parts[0][:rows, :]
    for e, part in enumerate(parts):
        rest[e] = part[rows:, :]
    for f, part in enumerate(sent):
        part[:rows, :] = first[:rows, :] - total
        part[rows:, :] = rest[(place[0] >> 1) ^ place[1] ^ f]


def last_kernel(place, *refs):
    *parts, high, low, own, other, last, joined = refs
    rows = own.shape[0]
    chip = place[0] >> 1
    for f, part in enumerate(parts):
        where = span(chip ^ f, GROUP)
        for n in range(4):
            joined[n, where, :] = part[n * GROUP : (n + 1) * GROUP, :]
        last[where, :] = part[rows:, :]
    columns = [jnp.concatenate([joined[n], joined[n + 1]], 0) for n in (0, 2)]
    values = product(jnp.concatenate(columns, 1), high[...], low[...], 1)
    own[...] = values[:rows]
    other[...] = values[rows:]


def part_kernel(place, *refs):
    own, other, last, kept, sent = refs
    total = own[...] + other[...]
    half = total.shape[1] // 2
    lower = (place[0] & 1) == 0
    for n, panel in enumerate((total, last[...])):
        own, other = panel[:, :half], panel[:, half:]
        if n:
            own, other = jnp.where(lower, own, other), jnp.where(lower, other, own)
        kept[:, n * half : (n + 1) * half] = own
        sent[:, n * half : (n + 1) * half] = other


def merge_kernel(place, kept, received, result):
    panels, half = result.shape[1:]
    lower = (place[0] & 1) == 0
    for chip in range(kept.shape[0] // GROUP):
        rows = slice(chip * GROUP, (chip + 1) * GROUP)
        for n in range(panels):
            columns = slice(n * half, (n + 1) * half)
            own, other = kept[rows, columns], received[rows, columns]
            start = 2 * chip * GROUP
            result[start : start + GROUP, n, :] = jnp.where(lower, own, other)
            result[start + GROUP : start + 2 * GROUP, n, :] = jnp.where(lower, other, own)


def reduce_blocks(ready, level, live, links, blocks, inverse, coupling, solved):
    red_blocks, link_total, size = inverse.shape[0], coupling.shape[1], inverse.shape[1]
    lanes = lax.broadcasted_iota(jnp.int32, (1, size), 1)
    values = []
    for i in range(red_blocks):
        mask = (lanes + i * size < live[0, level]).astype(jnp.float32)
        value = product(blocks[i] * mask, *halves(inverse[i]), 0) * mask
        solved[:, i * size : (i + 1) * size] = value
        values.append(value)
    ready()
    pushed = []
    for i in range(red_blocks):
        pairs = [halves(coupling[i, k]) for k in range(link_total)]
        high, low = (jnp.concatenate(part, 1) for part in zip(*pairs, strict=True))
        pushed.append(product(values[i], high, low, 0))
    for i in range(red_blocks):
        for k in range(link_total):
            target = red_blocks + links[i, k]
            blocks[target] = blocks[target] - pushed[i][:, k * size : (k + 1) * size]


def send_halves(place, level, blocks, red_blocks, kept, sent):
    half = kept.shape[0]
    upper = (place[0] >> level) & 1
    kept[...] = blocks[pl.ds(red_blocks + upper * half, half)]
    sent[...] = blocks[pl.ds(red_blocks + (1 - upper) * half, half)]


def load_halves(place, level, order, kept, received, joined, blocks):
    half = kept.shape[0]
    upper = (place[0] >> level) & 1
    joined[pl.ds(upper * half, half)] = kept[...]
    joined[pl.ds((1 - upper) * half, half)] = received[...]
    for n in range(2 * half):
        blocks[n] = joined[order[0, n]]


def lowest_kernel(place, live, links, section, inverse, coupling, solved, kept, sent, blocks):
    size = inverse.shape[1]
    for n in range(blocks.shape[0]):
        blocks[n] = section[:, n * size : (n + 1) * size]
    reduce_blocks(place[2], 0, live, links, blocks, inverse, coupling, solved)
    send_halves(place, 0, blocks, inverse.shape[0], kept, sent)


def middle_kernel(
    place, live, links, order, old, received, inverse, coupling, solved, kept, sent, joined, blocks
):
    load_halves(place, 0, order, old, received, joined, blocks)
    reduce_blocks(place[2], 1, live, links, blocks, inverse, coupling, solved)
    send_halves(place, 1, blocks, inverse.shape[0], kept, sent)


def highest_kernel(
    place, live, links, order, last_order, old, received, inverse, coupling, solved, kept, sent, joined, blocks
):
    load_halves(place, 1, order, old, received, joined, blocks)
    reduce_blocks(place[2], 2, live, links, blocks, inverse, coupling, solved)
    red_blocks, size = inverse.shape[0], inverse.shape[1]
    core = place[0] & 1
    for n in range(blocks.shape[0] - red_blocks):
        block = red_blocks + last_order[0, n]
        columns = slice(n * size, (n + 1) * size)
        for chip in range(kept.shape[0] // GROUP):
            rows = slice(chip * GROUP, (chip + 1) * GROUP)
            kept[rows, columns] = blocks[block, span(2 * chip + core, GROUP), :]
            sent[rows, columns] = blocks[block, span(2 * chip + 1 - core, GROUP), :]


def swap_chips(parts):
    return [parts[0]] + [flip(parts[f], "leaf", 2 * f) for f in range(1, len(parts))]


def solve_tree(right_sides, level_data, front_rows, root_inverse, root_coupling):
    leaf_count, col_count = lax.axis_size("leaf"), lax.axis_size("col")
    chip_count = leaf_count // 2
    panel_count, panel_rows, own_columns = root_inverse.shape
    group = GROUP * col_count
    rhs_rows = right_sides.shape[0]
    front_rows = front_rows.reshape(1, -1)
    red_blocks, size = level_data[0][0].shape[:2]
    solved = ((rhs_rows, red_blocks * size), jnp.float32)
    pair = ((2 * panel_rows, own_columns), jnp.bfloat16)
    wide = ((2 * panel_rows, 2 * own_columns), jnp.bfloat16)
    one = ((group, own_columns), jnp.float32)
    more = ((group + GROUP, own_columns), jnp.float32)
    both = ((group, panel_count * panel_rows), jnp.float32)

    def halved(count):
        return (((count - red_blocks) // 2, rhs_rows, size), jnp.float32)

    def scratch(*shape):
        return pltpu.VMEM(shape, jnp.float32)

    inverse, coupling, links, order = level_data[0]
    count = right_sides.shape[1] // size
    solved_first, kept, sent, second, first = kernel_call(
        lowest_kernel,
        [solved, halved(count), halved(count)],
        [front_rows, links],
        [],
        loaded=[right_sides, inverse, coupling],
        late=1,
        stacks=[[(root_inverse, 1)], [(root_inverse, 0)]],
        scratch=[scratch(count, rhs_rows, size)],
        room=64,
    )
    received = flip(sent, "leaf", 1)
    far = flip(root_coupling, "leaf", 4)
    second_far = flip(second, "leaf", 4)
    near = flip(root_coupling, "leaf", 2)
    first = flip(first, "col", 1)
    partner_inverse = flip(root_inverse, "leaf", 1)
    partner_coupling = flip(root_coupling, "leaf", 1)
    inverse, coupling, links, next_order = level_data[1]
    count -= red_blocks
    solved_second, kept, sent, second = kernel_call(
        middle_kernel,
        [solved, halved(count), halved(count)],
        [front_rows, links, order],
        [],
        loaded=[kept, received, inverse, coupling],
        late=1,
        stacks=[[(root_inverse, 1)]],
        held=[partner_inverse, partner_coupling],
        scratch=[scratch(count, rhs_rows, size)] * 2,
        room=64,
    )
    received = flip(sent, "leaf", 2)
    inverse, coupling, links, last_order = level_data[2]
    count -= red_blocks
    solved_third, kept, sent, near = kernel_call(
        highest_kernel,
        [solved, both, both],
        [front_rows, links, next_order, last_order],
        [],
        loaded=[kept, received, inverse, coupling],
        late=1,
        stacks=[[near]],
        held=[far],
        scratch=[scratch(count, rhs_rows, size)] * 2,
        room=64,
    )
    received = flip(sent, "leaf", 1)
    corner = flip(near, "leaf", 4)
    second_near = flip(second, "leaf", 2)
    (joined,) = kernel_call(join_kernel, [both], [], [kept, received], held=[second_far, first])

    near_high, near_low = kernel_call(pair_kernel, [pair, pair], [], [], loaded=[(root_inverse, 0), (partner_inverse, 0)])
    parts = swap_columns([joined] * col_count)
    parts = kernel_call(
        first_kernel,
        [more] * chip_count,
        [],
        [*parts, near_high, near_low, kept, received],
        held=[corner, second_near],
        scratch=[scratch(col_count, group, own_columns)],
    )
    corner, far = gate([corner, far], [parts[-1]])
    partner_corner = flip(corner, "leaf", 1)
    partner_far = flip(far, "leaf", 1)
    parts = swap_chips(parts)
    parts = kernel_call(
        share_kernel,
        [more] * col_count,
        [],
        parts,
        held=[partner_corner],
        scratch=[scratch(chip_count, GROUP, own_columns)],
    )
    second_near, near = gate([second_near, near], [parts[-1]])
    second_corner = flip(second_near, "leaf", 4)
    partner_near = flip(near, "leaf", 1)
    *between, sides = assemble(
        [(root_coupling, None), (near, 0), (far, None), (corner, 0)]
        + [(partner_coupling, None), (partner_near, 0), (partner_far, None), (partner_corner, 0)],
        stacks=[[second_near, second_far]],
    )
    parts = swap_columns(parts)
    left, first_sum = kernel_call(coupled_kernel, [one, one], [], [*parts, *between])
    sides, second_corner = gate([sides, second_corner], [left])
    partner_sides = flip(sides, "leaf", 1)
    panel = assemble(
        [(root_inverse, 1), (sides, 0), (sides, 1), (second_corner, 0)]
        + [(partner_inverse, 1), (partner_sides, 0), (partner_sides, 1)]
        + [(flip(second_corner, "leaf", 1), 0)]
    )
    parts = swap_columns([left] * col_count)
    parts = kernel_call(turn_kernel, [one] * col_count, [], [*parts, *panel])
    parts = swap_columns(parts)
    parts = kernel_call(back_kernel, [more] * col_count, [], [*parts, *between])
    parts = swap_columns(parts)
    parts = kernel_call(
        spread_kernel,
        [more] * chip_count,
        [],
        [*parts, first_sum],
        scratch=[scratch(col_count, GROUP, own_columns)],
    )
    (first,) = gate([first], [parts[-1]])
    first_high, first_low = kernel_call(
        pair_kernel,
        [wide, wide],
        [],
        [],
        loaded=[(root_inverse, 0), (partner_inverse, 0), (first, 0), (flip(first, "leaf", 1), 0)],
    )
    own, other, last = kernel_call(
        last_kernel,
        [one, one, one],
        [],
        [*swap_chips(parts), first_high, first_low],
        scratch=[scratch(col_count, group, own_columns)],
    )
    kept, sent = kernel_call(part_kernel, [both, both], [], [own, flip(other, "col", 2), last])
    (result,) = kernel_call(
        merge_kernel,
        [((rhs_rows, panel_count, panel_rows), jnp.float32)],
        [],
        [kept, flip(sent, "leaf", 1)],
    )
    return (solved_first, solved_second, solved_third, result)


def replicates(rhs_rows, root_inverse):
    leaf_count, col_count = lax.axis_size("leaf"), lax.axis_size("col")
    panel_rows, own_columns = root_inverse.shape[1:]
    return (
        leaf_count == 8
        and col_count == 4
        and rhs_rows == GROUP * leaf_count
        and own_columns == 2 * panel_rows
    )


def local(
    right_sides,
    inverse_first,
    coupling_first,
    links_first,
    order_first,
    inverse_second,
    coupling_second,
    links_second,
    order_second,
    inverse_third,
    coupling_third,
    links_third,
    order_third,
    front_rows,
    root_inverse,
    root_coupling,
):
    level_data = (
        (inverse_first, coupling_first, links_first, order_first),
        (inverse_second, coupling_second, links_second, order_second),
        (inverse_third, coupling_third, links_third, order_third),
    )
    if replicates(right_sides.shape[0], root_inverse):
        return solve_tree(right_sides, level_data, front_rows, root_inverse, root_coupling)
    section = right_sides
    outputs = []
    for level_index in range(3):
        inverse, coupling, link_ids, order_map = level_data[level_index]
        solved, skeleton = eliminate(
            section, inverse, coupling, link_ids, front_rows[level_index, 0]
        )
        outputs.append(solved)
        if level_index < 2:
            skeleton = join_halves(skeleton, level_index)
        skeleton = jnp.take(skeleton, order_map[0], axis=1)
        section = skeleton.reshape(skeleton.shape[0], -1)
    return (*outputs, root_wide(section, root_inverse, root_coupling))


def solution(mesh):
    in_specs = (
        P("col", "leaf"),
        P("leaf", None, None),
        P("leaf", None, None, None),
        P("leaf", None),
        P("leaf", None),
        P("leaf", None, None),
        P("leaf", None, None, None),
        P("leaf", None),
        P("leaf", None),
        P("leaf", None, None),
        P("leaf", None, None, None),
        P("leaf", None),
        P("leaf", None),
        P(None, "leaf"),
        P(None, "leaf", "col"),
        P("leaf", "col"),
    )
    out_specs = (P("col", "leaf"), P("col", "leaf"), P("col", "leaf"), P("col", None, "leaf"))
    return jax.shard_map(local, mesh=mesh, in_specs=in_specs, out_specs=out_specs, check_vma=False)
```
